32 devices in a mesh: dp: 16 (over z, x, core), tensor: 2 (over y).
Axes of the slice: x: 2, y: 2, z: 4, core: 2. Of those that a mesh axis runs over, the one named last changes fastest.
Arguments:
- tokens: bfloat16 [16384, 1024], P('dp'), may hold values from -6 to 6
- qkv_weight: bfloat16 [1024, 3, 1024], P(None, None, 'tensor'), may hold values from -0.1875 to 0.1875
- qkv_bias: bfloat16 [3, 1024], P(None, 'tensor'), may hold values from -1.75 to 1.75
- dense_weight: bfloat16 [1024, 1024], P('tensor'), may hold values from -3 to 3
- dense_bias: bfloat16 [1024], replicated, may hold values from -1.75 to 1.75
- fc1_weight: bfloat16 [1024, 4096], P(None, 'tensor'), may hold values from -0.1875 to 0.1875
- fc1_bias: bfloat16 [4096], P('tensor'), may hold values from -3 to 3
- fc2_weight: bfloat16 [4096, 1024], P('tensor'), may hold values from -0.09375 to 0.09375
- fc2_bias: bfloat16 [1024], replicated, may hold values from -1.75 to 1.75
- ln1_gain: bfloat16 [1024], replicated, may hold values from 0.099609375 to 1.8984375
- ln1_bias: bfloat16 [1024], replicated, may hold values from -1.75 to 1.75
- ln2_gain: bfloat16 [1024], replicated, may hold values from 0.099609375 to 1.8984375
- ln2_bias: bfloat16 [1024], replicated, may hold values from -1.75 to 1.75
- cotangent: bfloat16 [16384, 1024], P('dp'), may hold values from -18 to 18
Outputs:
- mixed: bfloat16 [16384, 1024], P('dp')
- input_grad: bfloat16 [16384, 1024], P('dp')
- qkv_weight_grad: float32 [1024, 3, 1024], P(None, None, 'tensor')
- qkv_bias_grad: float32 [3, 1024], P(None, 'tensor')
- dense_weight_grad: float32 [1024, 1024], P('tensor')
- dense_bias_grad: float32 [1024], replicated
- fc1_weight_grad: float32 [1024, 4096], P(None, 'tensor')
- fc1_bias_grad: float32 [4096], P('tensor')
- fc2_weight_grad: float32 [4096, 1024], P('tensor')
- fc2_bias_grad: float32 [1024], replicated
- ln1_gain_grad: float32 [1024], replicated
- ln1_bias_grad: float32 [1024], replicated
- ln2_gain_grad: float32 [1024], replicated
- ln2_bias_grad: float32 [1024], replicated
The draws below stay inside these ranges and needn't reach their ends.
All inputs are finite; a program needn't handle non-finite values.
Results may differ from the reference program's by a relative error of at most 0.012.
Values sent between devices are 32-bit elements; how exact they have to be, the bound alone decides.
A program may use at most 256 MiB of HBM per device.

```python
import jax
import jax.numpy as jnp
from jax import lax

D = 1024
HEADS = 16
HEAD_DIM = 64
FF = 4096
ROT_DIM = 16
LENGTH = 1024
TOKENS = 16384


def draw_cotangent(key, part):
    key = jax.random.fold_in(key, 11)
    seq_total = TOKENS // LENGTH
    places = (jnp.arange(TOKENS) // LENGTH).astype(jnp.float32)
    row_scale = jnp.exp(jnp.log(3.0) * places / max(seq_total - 1, 1))
    entries = jnp.clip(jax.random.normal(key, (TOKENS, D), jnp.float32), -6.0, 6.0)
    return (entries * row_scale[:, None]).astype(jnp.bfloat16)


def steps_of(rng, shape, shards, least, largest):
    loudness = 1.0
    for dim, shards_of in shards:
        steps = jax.random.uniform(jax.random.fold_in(jax.random.fold_in(rng, 6), dim), (shards_of,), jnp.float32, least / len(shards), largest / len(shards))
        loudness = loudness * jnp.repeat(jnp.exp(steps), shape[dim] // shards_of).reshape((-1,) + (1,) * (len(shape) - 1 - dim))
    return loudness


def scatter_about(stream_key, extent, width, bound, shards=(), kind=jnp.bfloat16):
    loudness = steps_of(stream_key, extent, shards, -0.22, 0.18) if shards else 1.0
    array = jax.random.normal(stream_key, extent, jnp.float32) * width * loudness
    return jnp.minimum(jnp.maximum(array, -bound), bound).astype(kind)


def setup_inputs(seed: int = 0) -> dict:
    key_list = jax.random.split(jax.random.key(seed), 15)
    tokens = scatter_about(key_list[0], (TOKENS, D), 1.0, 6.0, ((0, 16),))
    qkv_weight = scatter_about(key_list[1], (D, 3, D), D ** -0.5, 0.1875, ((2, 2),))
    qkv_bias = scatter_about(key_list[2], (3, D), 0.3, 1.75, ((1, 2),))
    dense_weight = scatter_about(key_list[3], (D, D), (max(D // 256, 1)) ** -0.5, 3.0, ((0, 2),))
    dense_bias = scatter_about(key_list[4], (D,), 0.3, 1.75)
    fc1_weight = scatter_about(key_list[5], (D, FF), D ** -0.5, 0.1875, ((1, 2),))
    fc1_bias = scatter_about(key_list[6], (FF,), 0.5, 3.0, ((0, 2),))
    fc2_weight = scatter_about(key_list[7], (FF, D), FF ** -0.5, 0.09375, ((0, 2),))
    fc2_bias = scatter_about(key_list[8], (D,), 0.3, 1.75)
    ln1_gain = jnp.clip(1.0 + 0.18 * jax.random.normal(key_list[9], (D,), jnp.float32), 0.099609375, 1.8984375).astype(jnp.bfloat16)
    ln1_bias = scatter_about(key_list[10], (D,), 0.3, 1.75)
    ln2_gain = jnp.clip(1.0 + 0.18 * jax.random.normal(key_list[11], (D,), jnp.float32), 0.099609375, 1.8984375).astype(jnp.bfloat16)
    ln2_bias = scatter_about(key_list[12], (D,), 0.3, 1.75)
    cotangent = draw_cotangent(jax.random.fold_in(key_list[14], 71), 0)
    return {"tokens": tokens, "qkv_weight": qkv_weight, "qkv_bias": qkv_bias, "dense_weight": dense_weight, "dense_bias": dense_bias, "fc1_weight": fc1_weight, "fc1_bias": fc1_bias, "fc2_weight": fc2_weight, "fc2_bias": fc2_bias, "ln1_gain": ln1_gain, "ln1_bias": ln1_bias, "ln2_gain": ln2_gain, "ln2_bias": ln2_bias, "cotangent": cotangent}


HIGHEST = lax.Precision.HIGHEST
EPS = 1e-05

@jax.custom_vjp
def low(v):
    return lax.optimization_barrier(v.astype(jnp.bfloat16)).astype(jnp.float32)

@jax.custom_vjp
def low_back(v):
    return v

def low_keep(v):
    return (low(v), None)

def low_pass(kept, grad):
    return (grad,)

def back_keep(v):
    return (v, None)

def back_low(kept, grad):
    return (low(grad),)
low.defvjp(low_keep, low_pass)
low_back.defvjp(back_keep, back_low)

def layer_norm(values, gain, offset):
    centered = values - lax.optimization_barrier(jnp.mean(values, -1, keepdims=True))
    variance = lax.optimization_barrier(jnp.mean(centered * centered, -1, keepdims=True))
    return centered * lax.rsqrt(variance + EPS) * gain + offset

def rotary_tables():
    places = jnp.arange(LENGTH, dtype=jnp.float32)
    rates = 10000.0 ** (-jnp.arange(0, ROT_DIM, 2, dtype=jnp.float32) / ROT_DIM)
    angles = places[:, None] * rates[None, :]
    return (jnp.cos(angles)[:, None, :], jnp.sin(angles)[:, None, :])

def rotate(values, cosine, sine):
    half_rot = ROT_DIM // 2
    lower = values[..., :half_rot]
    upper = values[..., half_rot:ROT_DIM]
    return jnp.concatenate([lower * cosine - upper * sine, upper * cosine + lower * sine, values[..., ROT_DIM:]], -1)

def attention_ref(queries, keys, values):
    block_rows = min(512, LENGTH)
    block_count = LENGTH // block_rows
    scale = HEAD_DIM ** (-0.5)
    query_blocks = queries.reshape(block_count, block_rows, HEADS, HEAD_DIM)
    starts = jnp.arange(block_count, dtype=jnp.int32) * block_rows
    columns = jnp.arange(LENGTH, dtype=jnp.int32)

    def one_block(operands):
        query_rows, block_start = operands
        scores = jnp.einsum('qhe,khe->hqk', query_rows, keys, precision=HIGHEST) * scale
        scores = low_back(scores)
        rows_here = block_start + jnp.arange(block_rows, dtype=jnp.int32)
        scores = jnp.where((rows_here[:, None] >= columns[None, :])[None], scores, -jnp.inf)
        probs = low(jax.nn.softmax(scores, -1))
        return jnp.einsum('hqk,khe->qhe', probs, values, precision=HIGHEST)
    outputs = lax.map(jax.checkpoint(one_block), (query_blocks, starts))
    return outputs.reshape(LENGTH, HEADS, HEAD_DIM)

def layer_forward(sequence, params):
    qkv_weight, qkv_bias, dense_weight, dense_bias, fc1_weight, fc1_bias, fc2_weight, fc2_bias, ln1_gain, ln1_bias, ln2_gain, ln2_bias = params
    first = low(layer_norm(sequence, ln1_gain, ln1_bias))
    second = low(layer_norm(sequence, ln2_gain, ln2_bias))
    projected = jnp.einsum('td,dcf->tcf', first, qkv_weight, precision=HIGHEST) + qkv_bias[None]
    projected = low_back(projected)
    cosine, sine = rotary_tables()
    head_shape = (LENGTH, HEADS, HEAD_DIM)
    queries = low(rotate(projected[:, 0].reshape(head_shape), cosine, sine))
    keys = low(rotate(projected[:, 1].reshape(head_shape), cosine, sine))
    values = low(projected[:, 2].reshape(head_shape))
    attended = attention_ref(queries, keys, values).reshape(LENGTH, D)
    attended = low(low_back(attended))
    attn_out = jnp.dot(attended, dense_weight, precision=HIGHEST)
    hidden = low_back(jnp.dot(second, fc1_weight, precision=HIGHEST) + fc1_bias)
    activated = low(jax.nn.gelu(hidden, approximate=False))
    mlp_out = jnp.dot(activated, fc2_weight, precision=HIGHEST)
    return sequence + attn_out + mlp_out + dense_bias + fc2_bias

def reference(tokens, qkv_weight, qkv_bias, dense_weight, dense_bias, fc1_weight, fc1_bias, fc2_weight, fc2_bias, ln1_gain, ln1_bias, ln2_gain, ln2_bias, cotangent):
    params = tuple((weight_in.astype(jnp.float32) for weight_in in (qkv_weight, qkv_bias, dense_weight, dense_bias, fc1_weight, fc1_bias, fc2_weight, fc2_bias, ln1_gain, ln1_bias, ln2_gain, ln2_bias)))
    inputs_all = tokens.astype(jnp.float32).reshape(-1, LENGTH, D)
    tangents_all = cotangent.astype(jnp.float32).reshape(-1, LENGTH, D)
    zero_totals = jax.tree.map(jnp.zeros_like, params)

    def accumulate(totals, seq_pair):
        sequence, tangent = seq_pair
        result, pullback = jax.vjp(layer_forward, sequence, params)
        seq_input_grad, param_grads = pullback(tangent)
        totals = jax.tree.map(jnp.add, totals, param_grads)
        return (totals, (result.astype(jnp.bfloat16), seq_input_grad.astype(jnp.bfloat16)))
    totals, (mixed, input_grad) = lax.scan(accumulate, zero_totals, (inputs_all, tangents_all))
    return (mixed.reshape(-1, D), input_grad.reshape(-1, D), totals[0], totals[1], totals[2], totals[3], totals[4], totals[5], totals[6], totals[7], totals[8], totals[9], totals[10], totals[11])
```

```python
import functools

import jax
import jax.numpy as jnp
import numpy as np
from jax import lax
from jax.experimental import pallas as pl
from jax.experimental.pallas import tpu as pltpu
from jax.sharding import PartitionSpec as P

HEAD_DIM = 64
ROT_DIM = 16
EPS = 1e-05
F32 = jnp.float32
BF16 = jnp.bfloat16
MESH = pl.DeviceIdType.MESH

GROUP = 16
UNIT = 64
LAG = 2
SLOTS = 8
CHUNK = 256


def rotary_tables(length):
    places = np.arange(length, dtype=np.float64)
    rates = 10000.0 ** (-np.arange(0, ROT_DIM, 2, dtype=np.float64) / ROT_DIM)
    angles = places[:, None] * rates[None, :]
    cosine = np.ones((length, 2 * HEAD_DIM), np.float32)
    sine = np.zeros((length, 2 * HEAD_DIM), np.float32)
    for start in (0, 8, HEAD_DIM, HEAD_DIM + 8):
        cosine[:, start : start + 8] = np.cos(angles)
        sine[:, start : start + 8] = np.sin(angles)
    return cosine, sine


def nn(left, right):
    return lax.dot_general(
        left, right, (((1,), (0,)), ((), ())), preferred_element_type=F32
    )


def nt(left, right):
    return lax.dot_general(
        left, right, (((1,), (1,)), ((), ())), preferred_element_type=F32
    )


def remote(src, dst, send, recv, device):
    return pltpu.make_async_remote_copy(
        src_ref=src,
        dst_ref=dst,
        send_sem=send,
        recv_sem=recv,
        device_id=device,
        device_id_type=MESH,
    )


def aligned(value, multiple):
    return pl.multiple_of(value, multiple)


class Place:
    def __init__(self):
        index = lax.axis_index("dp")
        base = index - lax.rem(index, GROUP)
        self.core = lax.rem(index, 2)
        self.x = lax.rem(index // 2, 2)
        z = lax.rem(index // 4, 4)

        def at(line, pair, core):
            return {"dp": base + (line * 2 + pair) * 2 + core}

        self.middle = (z == 1) | (z == 2)
        self.end = jnp.logical_not(self.middle)
        self.half = z // 2
        self.to_core = at(z, self.x, 1 - self.core)
        self.to_x = at(z, 1 - self.x, self.core)
        self.to_middle = at(jnp.where(z == 0, 1, 2), self.x, self.core)
        self.to_end = at(jnp.where(z == 1, 0, 3), self.x, self.core)
        self.to_pair = at(jnp.where(z == 1, 2, 1), self.x, self.core)
        self.to_y = {"tensor": 1 - lax.axis_index("tensor")}

    def meet(self):
        barrier = pltpu.get_barrier_semaphore()

        def signal(device):
            pl.semaphore_signal(barrier, inc=1, device_id=device, device_id_type=MESH)

        signal(self.to_core)
        signal(self.to_x)
        signal(self.to_y)

        @pl.when(self.middle)
        def _():
            signal(self.to_end)
            signal(self.to_pair)
            pl.semaphore_wait(barrier, 5)

        @pl.when(self.end)
        def _():
            signal(self.to_middle)
            pl.semaphore_wait(barrier, 4)


def all_reduce_step(step, units, place, total, slots, send, recv, finish):
    quarter = UNIT // 4
    x, half = place.x, place.half
    slot_x, slot_ae, slot_be, slot_am, slot_bm, slot_bx, slot_af = slots

    def rows(unit, offset, count):
        return total.at[pl.ds(aligned(unit * UNIT + offset, 8), count)]

    def part_a(unit, which):
        return rows(unit, which * quarter, quarter)

    def part_b(unit, which):
        return rows(unit, 2 * quarter + which * quarter, quarter)

    def whole_b(unit):
        return rows(unit, 2 * quarter, 2 * quarter)

    def copy(kind, slot, src, dst, device):
        return remote(src, dst, send.at[kind, slot], recv.at[kind, slot], device)

    def stage(number, condition=None):
        unit = step - 1 - (number - 1) * LAG
        active = (unit >= 0) & (unit < units)
        if condition is not None:
            active = active & condition

        def run(body):
            @pl.when(active)
            def _():
                body(unit, lax.rem(unit, SLOTS))

        return run

    def x_halves(u, s):
        return copy(0, s, part_a(u, 1 - x), slot_x.at[s], place.to_x)

    def a_to_middle(u, s):
        return copy(1, s, part_a(u, x), slot_ae.at[s], place.to_middle)

    def b_to_middle(u, s):
        return copy(2, s, whole_b(u), slot_be.at[s], place.to_middle)

    def a_exchange(u, s):
        return copy(3, s, part_a(u, x), slot_am.at[s], place.to_pair)

    def b_halves(u, s):
        return copy(4, s, part_b(u, 1 - half), slot_bm.at[s], place.to_pair)

    def b_exchange(u, s):
        return copy(5, s, part_b(u, half), slot_bx.at[s], place.to_x)

    def a_to_end(u, s):
        return copy(6, s, part_a(u, x), slot_af.at[s], place.to_end)

    def b_to_pair(u, s):
        return copy(7, s, part_b(u, half), part_b(u, half), place.to_pair)

    def b_to_end(u, s):
        return copy(8, s, whole_b(u), whole_b(u), place.to_end)

    def a_to_x(u, s):
        return copy(9, s, part_a(u, x), part_a(u, x), place.to_x)

    @stage(6, place.middle)
    def _(u, s):
        b_to_end(u, s).wait_send()

    @stage(6, place.end)
    def _(u, s):
        copy(8, s, whole_b(u), whole_b(u), place.to_middle).wait_recv()
        a_to_x(u, s).wait_send()

    @stage(6)
    def _(u, s):
        copy(9, s, part_a(u, 1 - x), part_a(u, 1 - x), place.to_x).wait_recv()
        finish(u)

    @stage(5, place.end)
    def _(u, s):
        copy(6, s, part_a(u, x), slot_af.at[s], place.to_middle).wait_recv()
        part_a(u, x)[...] = slot_af[s]
        a_to_x(u, s).start()

    @stage(5, place.middle)
    def _(u, s):
        copy(7, s, part_b(u, 1 - half), part_b(u, 1 - half), place.to_pair).wait_recv()
        b_to_end(u, s).start()
        a_to_end(u, s).wait_send()
        a_to_x(u, s).wait_send()
        b_to_pair(u, s).wait_send()

    @stage(3, place.end)
    def _(u, s):
        a_to_middle(u, s).wait_send()

    @stage(3, place.middle)
    def _(u, s):
        copy(1, s, part_a(u, x), slot_ae.at[s], place.to_end).wait_recv()
        b_halves(u, s).wait()
        part_a(u, x)[...] += slot_ae[s]
        a_exchange(u, s).start()
        part_b(u, half)[...] += slot_bm[s]
        b_exchange(u, s).start()

    @stage(4, place.middle)
    def _(u, s):
        a_exchange(u, s).wait()
        b_exchange(u, s).wait()
        part_a(u, x)[...] += slot_am[s]
        a_to_end(u, s).start()
        a_to_x(u, s).start()
        part_b(u, half)[...] += slot_bx[s]
        b_to_pair(u, s).start()

    @stage(2)
    def _(u, s):
        x_halves(u, s).wait()
        part_a(u, x)[...] += slot_x[s]

    @stage(2, place.end)
    def _(u, s):
        b_to_middle(u, s).wait_send()
        a_to_middle(u, s).start()

    @stage(2, place.middle)
    def _(u, s):
        copy(2, s, whole_b(u), slot_be.at[s], place.to_end).wait_recv()
        whole_b(u)[...] += slot_be[s]
        b_halves(u, s).start()

    @stage(1)
    def _(u, s):
        x_halves(u, s).start()

    @stage(1, place.end)
    def _(u, s):
        b_to_middle(u, s).start()


def rotated(values, cosine, sine, lane, direction):
    later = pltpu.roll(values, 2 * HEAD_DIM - 8, 1)
    earlier = pltpu.roll(values, 8, 1)
    turned = jnp.where(lane < 8, -direction * later, direction * earlier)
    return values * cosine + turned * sine


def layer_kernel(
    sizes,
    x_in,
    g_in,
    qkv_in,
    dense_in,
    fc1_in,
    fc2_in,
    vectors,
    fc1_bias,
    qkv_bias,
    cosine_in,
    sine_in,
    fc1_out,
    fc2_out,
    dense_out,
    qkv_out,
    small_out,
    branch_own,
    branch_other,
    norm_own,
    norm_other,
    total,
    stage,
    core_in,
    slot_x,
    slot_ae,
    slot_be,
    slot_am,
    slot_bm,
    slot_bx,
    slot_af,
    x_ref,
    g_ref,
    ln_ref,
    ln_t,
    branch,
    norm,
    fc1_ref,
    fc2_ref,
    qkv_ref,
    dense_ref,
    q_ref,
    k_ref,
    v_ref,
    kv_t,
    o_t,
    do_ref,
    dq_t,
    dk_ref,
    dv_ref,
    cosine,
    sine,
    act_t,
    hg_ref,
    lse,
    fc1_bias_sum,
    qkv_bias_sum,
    small,
    small_y,
    small_core,
    send,
    recv,
    core_send,
    core_recv,
    load_sem,
    weight_sem,
    out_sem,
    y_send,
    y_recv,
):
    tokens, width, local, hidden = sizes
    heads = local // HEAD_DIM
    chunks = hidden // CHUNK
    blocks = tokens // 256
    wide = width // 256
    place = Place()
    core = place.core
    fc_messages = 2 * chunks
    dense_messages = local // 256
    qkv_first = fc_messages + dense_messages
    qkv_messages = 3 * width * local // (256 * width)
    messages = qkv_first + qkv_messages
    units = messages * 128 // UNIT + 1
    small_unit = units - 1

    def load(src, dst, which):
        return pltpu.make_async_copy(src, dst, load_sem.at[which])

    def load_chunk(chunk):
        slot = lax.rem(chunk, 2)
        at = pl.ds(aligned(chunk * CHUNK, CHUNK), CHUNK)
        return (
            pltpu.make_async_copy(
                fc1_in.at[:, at], fc1_ref.at[slot], weight_sem.at[slot, 0]
            ),
            pltpu.make_async_copy(fc2_in.at[at], fc2_ref.at[slot], weight_sem.at[slot, 1]),
        )

    loads = [
        load(x_in, x_ref, 0),
        load(g_in, g_ref, 1),
        load(qkv_in, qkv_ref, 2),
        load(dense_in, dense_ref, 3),
        load(cosine_in, cosine, 4),
        load(sine_in, sine, 5),
    ]
    loads[0].start()
    for item in load_chunk(0):
        item.start()
    for item in loads[1:]:
        item.start()

    def row_block(index, size=256):
        return pl.ds(aligned(index * size, size), size)

    def normed_rows(rows):
        values = x_ref[rows, :].astype(F32)
        centered = values - jnp.mean(values, -1, keepdims=True)
        variance = jnp.mean(centered * centered, -1, keepdims=True)
        return centered * lax.rsqrt(variance + EPS)

    def normalise(gain, offset):
        def body(index, carry):
            rows = row_block(index, 128)
            low = (normed_rows(rows) * vectors[gain : gain + 1] + vectors[offset : offset + 1]).astype(
                BF16
            )
            ln_ref[rows, :] = low
            ln_t[:, rows] = low.T
            return carry

        lax.fori_loop(0, tokens // 128, body, 0)


    def core_copy(message):
        slot = lax.rem(message, 4)
        return remote(
            stage.at[slot, pl.ds(aligned((1 - core) * 128, 128), 128)],
            core_in.at[slot],
            core_send.at[slot],
            core_recv.at[slot],
            place.to_core,
        )

    def collect(message):
        core_copy(message).wait()
        slot = lax.rem(message, 4)

        def body(index, carry):
            at = pl.ds(aligned(index * 32, 32), 32)
            own = stage[slot, pl.ds(aligned(core * 128 + index * 32, 32), 32)]
            total[pl.ds(aligned(message * 128 + index * 32, 32), 32)] = own + core_in[slot, at]
            return carry

        lax.fori_loop(0, 4, body, 0)


    def put(src, dst):
        pltpu.make_async_copy(src, dst, out_sem.at[0]).start()
        remote(src, dst, out_sem.at[1], out_sem.at[2], place.to_core).start()

    def finish(unit):
        message = unit // 2
        at = core * 128 + lax.rem(unit, 2) * UNIT
        rows = pl.ds(aligned(unit * UNIT, UNIT), UNIT)

        @pl.when((message < fc_messages) & (lax.rem(message, 2) == 0))
        def _():
            put(
                total.at[rows],
                fc2_out.at[pl.ds(aligned(message // 2 * CHUNK + at, UNIT), UNIT)],
            )

        @pl.when((message < fc_messages) & (lax.rem(message, 2) == 1))
        def _():
            columns = pl.ds(aligned(message // 2 * CHUNK, CHUNK), CHUNK)
            for part in range(wide):
                put(
                    total.at[rows, pl.ds(part * 256, 256)],
                    fc1_out.at[pl.ds(aligned(part * 256 + at, UNIT), UNIT), columns],
                )

        @pl.when((message >= fc_messages) & (message < qkv_first))
        def _():
            first = (message - fc_messages) * 256
            put(total.at[rows], dense_out.at[pl.ds(aligned(first + at, UNIT), UNIT)])

        @pl.when((message >= qkv_first) & (unit < small_unit))
        def _():
            which = message - qkv_first
            member = which // (width // 512)
            first = lax.rem(which, width // 512) * 256
            for part in range(width // local):
                put(
                    total.at[rows, pl.ds(part * local, local)],
                    qkv_out.at[member, pl.ds(aligned(part * 512 + first + at, UNIT), UNIT)],
                )

        @pl.when(unit == small_unit)
        def _():
            put(
                total.at[pl.ds(small_unit * UNIT, 8)],
                small_out.at[pl.ds(aligned(core * 8, 8), 8)],
            )


    def feed_forward(chunk):
        slot = lax.rem(chunk, 2)
        for item in load_chunk(chunk):
            item.wait()

        @pl.when(chunk < chunks - 1)
        def _():
            for item in load_chunk(chunk + 1):
                item.start()

        offset = fc1_bias[pl.ds(chunk, 1)]

        def body(index, bias_sum):
            rows = row_block(index)
            values = nn(ln_ref[rows, :], fc1_ref[slot]) + offset
            back = nt(g_ref[rows, :], fc2_ref[slot])
            share = 0.5 + 0.5 * lax.erf(values * 0.7071067811865476)
            act = (values * share).astype(BF16)
            slope = share + values * (
                jnp.exp(values * values * -0.5) * 0.3989422804014327
            )
            hg = (back * slope).astype(BF16)
            act_t[:, rows] = act.T
            hg_ref[rows, :] = hg
            branch[rows, :] += nn(act, fc2_ref[slot])
            norm[rows, :] += nt(hg, fc1_ref[slot])
            return bias_sum + jnp.sum(hg.astype(F32), 0, keepdims=True)

        bias_sum = lax.fori_loop(0, blocks, body, jnp.zeros((1, CHUNK), F32))
        fc1_bias_sum[pl.ds(chunk, 1)] = bias_sum
        message = 2 * chunk
        first, second = lax.rem(message, 4), lax.rem(message + 1, 4)

        def fc2_grad(index, carry):
            columns = row_block(index)
            stage[first, :, columns] = nn(act_t[...], g_ref[:, columns])
            return carry

        lax.fori_loop(0, wide, fc2_grad, 0)
        core_copy(message).start()

        def fc1_grad(index, carry):
            columns = row_block(index)
            stage[second, :, columns] = nn(ln_t[columns, :], hg_ref[...])
            return carry

        lax.fori_loop(0, wide, fc1_grad, 0)
        core_copy(message + 1).start()

    lane = lax.rem(lax.broadcasted_iota(jnp.int32, (256, 2 * HEAD_DIM), 1), HEAD_DIM)
    lane_head = lax.broadcasted_iota(jnp.int32, (256, 2 * HEAD_DIM), 1) // HEAD_DIM
    causal = lax.broadcasted_iota(jnp.int32, (256, 256), 0) <= lax.broadcasted_iota(
        jnp.int32, (256, 256), 1
    )

    def end_feed_forward():
        def body(index, sums):
            rows = row_block(index, 128)
            grad = norm[rows, :]
            norm[rows, :] = grad * vectors[2:3]
            return (
                sums[0] + jnp.sum(grad * normed_rows(rows), 0, keepdims=True),
                sums[1] + jnp.sum(grad, 0, keepdims=True),
                sums[2] + jnp.sum(g_ref[rows, :].astype(F32), 0, keepdims=True),
            )

        zero = jnp.zeros((1, width), F32)
        sums = lax.fori_loop(0, tokens // 128, body, (zero, zero, zero))
        small[10:11] = sums[0]
        small[11:12] = sums[1]
        small[0:1] = sums[2]
        normalise(0, 1)

    def project():
        for member, target in enumerate((q_ref, k_ref, v_ref)):

            def body(index, carry, member=member, target=target):
                rows = row_block(index)
                values = nn(ln_ref[rows, :], qkv_ref[member]) + qkv_bias[member : member + 1]
                for pair in range(heads // 2):
                    lanes = slice(pair * 128, pair * 128 + 128)
                    part = values[:, lanes]
                    if member < 2:
                        part = rotated(part, cosine[rows, :], sine[rows, :], lane, 1.0)
                    if member == 0:
                        part = part * HEAD_DIM**-0.5
                    target[rows, lanes] = part.astype(BF16)
                if member == 2:
                    kv_t[:, rows] = values.astype(BF16).T
                return carry

            lax.fori_loop(0, blocks, body, 0)

    def head_lanes(head):
        return pl.ds(aligned(head // 2 * 128, 128), 128)

    def one_head(values, head):
        return jnp.where(lane_head == lax.rem(head, 2), values, jnp.zeros_like(values))

    def attend(head):
        lanes = head_lanes(head)
        head_rows = pl.ds(aligned(head * HEAD_DIM, HEAD_DIM), HEAD_DIM)
        for block in range(blocks):
            start = block * 256
            rows = slice(start, start + 256)
            query = one_head(q_ref[rows, lanes], head)
            near = nt(k_ref[rows, lanes], query)
            near = jnp.where(causal, near, -jnp.inf)
            peak = jnp.max(near, 0, keepdims=True)
            if block:
                far = nt(k_ref[0:start, lanes], query)
                peak = jnp.maximum(peak, jnp.max(far, 0, keepdims=True))
            near = jnp.exp(near - peak)
            weight = jnp.sum(near, 0, keepdims=True)
            result = nn(kv_t[head_rows, rows], near.astype(BF16))
            if block:
                far = jnp.exp(far - peak)
                weight = weight + jnp.sum(far, 0, keepdims=True)
                result = result + nn(kv_t[head_rows, 0:start], far.astype(BF16))
            o_t[head_rows, rows] = (result / weight).astype(BF16)
            lse[pl.ds(head, 1), rows] = peak + jnp.log(weight)

    def branch_copy():
        return remote(branch, branch_other, y_send.at[0], y_recv.at[0], place.to_y)

    def norm_copy():
        return remote(norm, norm_other, y_send.at[1], y_recv.at[1], place.to_y)

    def small_copy():
        return remote(small.at[8:16], small_y, y_send.at[2], y_recv.at[2], place.to_y)

    def small_core_copy():
        return remote(
            small.at[pl.ds(aligned((1 - core) * 8, 8), 8)],
            small_core,
            y_send.at[3],
            y_recv.at[3],
            place.to_core,
        )

    def own_branch():
        return pltpu.make_async_copy(branch, branch_own, load_sem.at[0])

    def own_norm():
        return pltpu.make_async_copy(norm, norm_own, load_sem.at[1])

    def end_attend():
        def body(index, carry):
            rows = row_block(index)
            branch[rows, :] += nn(o_t[:, rows].T, dense_ref[...])
            return carry

        lax.fori_loop(0, blocks, body, 0)
        branch_copy().start()
        own_branch().start()
        for part in range(dense_messages):
            message = fc_messages + part

            def dense_grad(index, carry, part=part, message=message):
                columns = row_block(index)
                stage[message % 4, :, columns] = nn(
                    o_t[part * 256 : part * 256 + 256, :], g_ref[:, columns]
                )
                return carry

            lax.fori_loop(0, wide, dense_grad, 0)
            core_copy(message).start()

        def back(index, carry):
            rows = row_block(index)
            do_ref[rows, :] = nt(g_ref[rows, :], dense_ref[...]).astype(BF16)
            kv_t[:, rows] = k_ref[rows, :].T
            return carry

        lax.fori_loop(0, blocks, back, 0)

    def attend_back(head):
        lanes = head_lanes(head)
        head_rows = pl.ds(aligned(head * HEAD_DIM, HEAD_DIM), HEAD_DIM)

        @pl.when(lax.rem(head, 2) == 0)
        def _():
            dk_ref[...] = jnp.zeros_like(dk_ref)
            dv_ref[...] = jnp.zeros_like(dv_ref)

        for block in range(blocks):
            start = block * 256
            rows = slice(start, start + 256)
            query = one_head(q_ref[rows, lanes], head)
            grad = one_head(do_ref[rows, lanes], head)
            stat = lse[pl.ds(head, 1), rows]
            near = jnp.exp(jnp.where(causal, nt(k_ref[rows, lanes], query), -jnp.inf) - stat)
            near_back = nt(v_ref[rows, lanes], grad)
            centre = jnp.sum(near * near_back, 0, keepdims=True)
            if block:
                far = jnp.exp(nt(k_ref[0:start, lanes], query) - stat)
                far_back = nt(v_ref[0:start, lanes], grad)
                centre = centre + jnp.sum(far * far_back, 0, keepdims=True)
            dv_ref[rows, :] += nn(near.astype(BF16), grad)
            near = (near * (near_back - centre)).astype(BF16)
            dk_ref[rows, :] += nn(near, query)
            result = nn(kv_t[head_rows, rows], near)
            if block:
                dv_ref[0:start, :] += nn(far.astype(BF16), grad)
                far = (far * (far_back - centre)).astype(BF16)
                dk_ref[0:start, :] += nn(far, query)
                result = result + nn(kv_t[head_rows, 0:start], far)
            dq_t[head_rows, rows] = result

        @pl.when(lax.rem(head, 2) == 1)
        def _():
            def body(index, carry):
                rows = row_block(index)
                k_ref[rows, lanes] = rotated(
                    dk_ref[rows, :], cosine[rows, :], sine[rows, :], lane, -1.0
                ).astype(BF16)
                v_ref[rows, lanes] = dv_ref[rows, :].astype(BF16)
                return carry

            lax.fori_loop(0, blocks, body, 0)

    def end_back():
        def body(index, sums):
            rows = row_block(index)
            for pair in range(heads // 2):
                lanes = slice(pair * 128, pair * 128 + 128)
                part = dq_t[lanes, rows].T * HEAD_DIM**-0.5
                q_ref[rows, lanes] = rotated(
                    part, cosine[rows, :], sine[rows, :], lane, -1.0
                ).astype(BF16)
            members = [ref[rows, :] for ref in (q_ref, k_ref, v_ref)]
            grad = nt(members[0], qkv_ref[0])
            for member in (1, 2):
                grad = grad + nt(members[member], qkv_ref[member])
            norm[rows, :] += grad * vectors[0:1]
            return (
                sums[0] + jnp.sum(grad * normed_rows(rows), 0, keepdims=True),
                sums[1] + jnp.sum(grad, 0, keepdims=True),
                *(
                    total_here + jnp.sum(member.astype(F32), 0, keepdims=True)
                    for total_here, member in zip(sums[2:], members)
                ),
            )

        zero, zero_local = jnp.zeros((1, width), F32), jnp.zeros((1, local), F32)
        sums = lax.fori_loop(0, blocks, body, (zero, zero, zero_local, zero_local, zero_local))
        norm_copy().start()
        own_norm().start()
        small[8:9] = sums[0]
        small[9:10] = sums[1]
        for member in range(3):
            qkv_bias_sum[member : member + 1] = sums[2 + member]

    def qkv_grad(member, target):
        for which in range(width // 512):
            message = qkv_first + member * (width // 512) + which
            slot = lax.rem(message, 4)
            for part in range(width // local):
                first = part * 512 + which * 256
                stage[slot, :, part * local : part * local + local] = nn(
                    ln_t[first : first + 256, :], target[...]
                )
            core_copy(message).start()

    def gather_small():
        small[12:16] = jnp.zeros((4, width), F32)
        small[5:8] = jnp.zeros((3, width), F32)
        for part in range(hidden // CHUNK):
            row, at = part * CHUNK // width, part * CHUNK % width
            small[1 + row : 2 + row, at : at + CHUNK] = fc1_bias_sum[part : part + 1]
        for member in range(3):
            row, at = member * local // width, member * local % width
            small[3 + row : 4 + row, at : at + local] = qkv_bias_sum[member : member + 1]
        small[4:5, 512:1024] = jnp.zeros((1, 512), F32)
        small_copy().start()

    def small_cores():
        small_copy().wait()
        small[8:16] += small_y[...]
        small_core_copy().start()

    def end_small():
        small_core_copy().wait()
        total[pl.ds(small_unit * UNIT, UNIT)] = jnp.zeros((UNIT, width), F32)
        total[pl.ds(small_unit * UNIT, 8)] = (
            small[pl.ds(aligned(core * 8, 8), 8)] + small_core[...]
        )

    def clear(index, carry):
        rows = row_block(index, 128)
        branch[rows, :] = jnp.zeros((128, width), F32)
        norm[rows, :] = jnp.zeros((128, width), F32)
        return carry

    lax.fori_loop(0, tokens // 128, clear, 0)
    loads[0].wait()
    normalise(2, 3)
    for item in loads[1:]:
        item.wait()
    place.meet()

    fwd = chunks + 2
    back = fwd + heads // 2 + 1
    last = back + heads + 1
    steps = units + 1 + 5 * LAG

    def step_body(step, carry):

        @pl.when((step >= 1) & (step <= chunks))
        def _():
            collect(2 * step - 2)
            collect(2 * step - 1)

        @pl.when(step == back)
        def _():
            for part in range(dense_messages):
                collect(fc_messages + part)

        @pl.when((step > last) & (step <= last + 3))
        def _():
            per = width // 512
            for part in range(per):
                collect(qkv_first + (step - last - 1) * per + part)

        all_reduce_step(
            step,
            units,
            place,
            total,
            (slot_x, slot_ae, slot_be, slot_am, slot_bm, slot_bx, slot_af),
            send,
            recv,
            finish,
        )

        @pl.when(step < chunks)
        def _():
            feed_forward(step)

        @pl.when(step == chunks)
        def _():
            end_feed_forward()

        @pl.when(step == chunks + 1)
        def _():
            project()

        @pl.when((step >= fwd) & (step < fwd + heads // 2))
        def _():
            def both(index, carry):
                attend((step - fwd) * 2 + index)
                return carry

            lax.fori_loop(0, 2, both, 0)

        @pl.when(step == back - 1)
        def _():
            end_attend()

        @pl.when((step >= back) & (step < back + heads))
        def _():
            attend_back(step - back)

        @pl.when(step == last - 1)
        def _():
            end_back()

        for member, target in enumerate((q_ref, k_ref, v_ref)):

            @pl.when(step == last + member)
            def _(member=member, target=target):
                qkv_grad(member, target)

        @pl.when(step == last + 3)
        def _():
            gather_small()

        @pl.when(step == last + 4)
        def _():
            small_cores()

        @pl.when(step == last + 5)
        def _():
            end_small()

        return carry

    lax.fori_loop(0, steps, step_body, 0)

    done = total.at[pl.ds(0, small_unit * UNIT + 8)]
    pltpu.make_async_copy(done, done, out_sem.at[0]).wait()
    every = remote(done, done, out_sem.at[1], out_sem.at[2], place.to_core)
    every.wait_send()
    every.wait_recv()
    own_branch().wait()
    own_norm().wait()
    branch_copy().wait()
    norm_copy().wait()


def layer(tokens, cotangent, qkv_weight, dense_weight, fc1_weight, fc2_weight, vectors, fc1_bias, qkv_bias):
    rows, width = tokens.shape
    local, hidden = qkv_weight.shape[2], fc1_weight.shape[1]
    cosine, sine = (jnp.asarray(table) for table in rotary_tables(rows))
    hbm = pl.BlockSpec(memory_space=pl.ANY)
    vmem = pl.BlockSpec(memory_space=pltpu.VMEM)
    quarter = UNIT // 4
    chunks = hidden // CHUNK
    unit_rows = (2 * chunks + local // 256 + 3 * local // 256) * 128 + UNIT
    dma = pltpu.SemaphoreType.DMA
    scratch = [
        pltpu.VMEM((unit_rows, width), F32),
        pltpu.VMEM((4, 256, width), F32),
        pltpu.VMEM((4, 128, width), F32),
        pltpu.VMEM((SLOTS, quarter, width), F32),
        pltpu.VMEM((SLOTS, quarter, width), F32),
        pltpu.VMEM((SLOTS, 2 * quarter, width), F32),
        pltpu.VMEM((SLOTS, quarter, width), F32),
        pltpu.VMEM((SLOTS, quarter, width), F32),
        pltpu.VMEM((SLOTS, quarter, width), F32),
        pltpu.VMEM((SLOTS, quarter, width), F32),
        pltpu.VMEM((rows, width), BF16),
        pltpu.VMEM((rows, width), BF16),
        pltpu.VMEM((rows, width), BF16),
        pltpu.VMEM((width, rows), BF16),
        pltpu.VMEM((rows, width), F32),
        pltpu.VMEM((rows, width), F32),
        pltpu.VMEM((2, width, CHUNK), BF16),
        pltpu.VMEM((2, CHUNK, width), BF16),
        pltpu.VMEM((3, width, local), BF16),
        pltpu.VMEM((local, width), BF16),
        pltpu.VMEM((rows, local), BF16),
        pltpu.VMEM((rows, local), BF16),
        pltpu.VMEM((rows, local), BF16),
        pltpu.VMEM((local, rows), BF16),
        pltpu.VMEM((local, rows), BF16),
        pltpu.VMEM((rows, local), BF16),
        pltpu.VMEM((local, rows), F32),
        pltpu.VMEM((rows, 2 * HEAD_DIM), F32),
        pltpu.VMEM((rows, 2 * HEAD_DIM), F32),
        pltpu.VMEM((rows, 2 * HEAD_DIM), F32),
        pltpu.VMEM((rows, 2 * HEAD_DIM), F32),
        pltpu.VMEM((CHUNK, rows), BF16),
        pltpu.VMEM((rows, CHUNK), BF16),
        pltpu.VMEM((local // HEAD_DIM, rows), F32),
        pltpu.VMEM((chunks, CHUNK), F32),
        pltpu.VMEM((3, local), F32),
        pltpu.VMEM((16, width), F32),
        pltpu.VMEM((8, width), F32),
        pltpu.VMEM((8, width), F32),
        dma((10, SLOTS)),
        dma((10, SLOTS)),
        dma((4,)),
        dma((4,)),
        dma((6,)),
        dma((2, 2)),
        dma((3,)),
        dma((4,)),
        dma((4,)),
    ]
    out = jax.ShapeDtypeStruct
    return pl.pallas_call(
        functools.partial(layer_kernel, (rows, width, local, hidden)),
        out_shape=[
            out((width, hidden), F32),
            out((hidden, width), F32),
            out((local, width), F32),
            out((3, width, local), F32),
            out((16, width), F32),
            out((rows, width), F32),
            out((rows, width), F32),
            out((rows, width), F32),
            out((rows, width), F32),
        ],
        in_specs=[hbm] * 6 + [vmem] * 3 + [hbm] * 2,
        out_specs=[hbm] * 9,
        scratch_shapes=scratch,
        compiler_params=pltpu.CompilerParams(
            collective_id=0, has_side_effects=True, vmem_limit_bytes=63 * 2**20
        ),
    )(
        tokens,
        cotangent,
        jnp.transpose(qkv_weight, (1, 0, 2)),
        dense_weight,
        fc1_weight,
        fc2_weight,
        vectors,
        fc1_bias,
        qkv_bias,
        cosine,
        sine,
    )


def per_device(
    groups,
    tokens,
    qkv_weight,
    qkv_bias,
    dense_weight,
    dense_bias,
    fc1_weight,
    fc1_bias,
    fc2_weight,
    fc2_bias,
    ln1_gain,
    ln1_bias,
    ln2_gain,
    ln2_bias,
    cotangent,
):
    width = tokens.shape[1]
    local, hidden = qkv_weight.shape[2], fc1_weight.shape[1]
    chunks = hidden // CHUNK
    rows_of = jnp.stack([ln1_gain, ln1_bias, ln2_gain, ln2_bias]).astype(F32)
    fc1_grad, fc2_grad, dense_grad, qkv_grad, small, *shares = layer(
        tokens,
        cotangent,
        qkv_weight,
        dense_weight,
        fc1_weight,
        fc2_weight,
        rows_of,
        fc1_bias.astype(F32).reshape(chunks, CHUNK),
        qkv_bias.astype(F32),
    )
    if groups is not None:
        fc1_grad, fc2_grad, dense_grad, qkv_grad, small = lax.psum(
            (fc1_grad, fc2_grad, dense_grad, qkv_grad, small), "dp", axis_index_groups=groups
        )
    branch_own, branch_other, norm_own, norm_other = shares
    residual = tokens.astype(F32)
    mixed = (
        residual
        + (branch_own + branch_other)
        + dense_bias.astype(F32)
        + fc2_bias.astype(F32)
    ).astype(BF16)
    centered = residual - jnp.mean(residual, -1, keepdims=True)
    inv_std = lax.rsqrt(jnp.mean(centered * centered, -1, keepdims=True) + EPS)
    normed = centered * inv_std
    scaled = norm_own + norm_other
    input_grad = cotangent.astype(F32) + inv_std * (
        scaled
        - jnp.mean(scaled, -1, keepdims=True)
        - normed * jnp.mean(scaled * normed, -1, keepdims=True)
    )
    flat = small.reshape(-1)
    bias_grad = small[0]
    return (
        mixed,
        input_grad.astype(BF16),
        jnp.transpose(qkv_grad, (1, 0, 2)),
        flat[3 * width : 3 * width + 3 * local].reshape(3, local),
        dense_grad,
        bias_grad,
        fc1_grad,
        flat[width : width + hidden],
        fc2_grad,
        bias_grad,
        small[8],
        small[9],
        small[10],
        small[11],
    )


def solution(mesh):
    dp = mesh.shape["dp"]
    groups = None
    if dp > GROUP:
        groups = [[start + i for start in range(0, dp, GROUP)] for i in range(GROUP)]
    placed = (
        P("dp", None),
        P(None, None, "tensor"),
        P(None, "tensor"),
        P("tensor", None),
        P(),
        P(None, "tensor"),
        P("tensor"),
        P("tensor", None),
        P(),
        P(),
        P(),
        P(),
        P(),
        P("dp", None),
    )
    return jax.shard_map(
        functools.partial(per_device, groups),
        mesh=mesh,
        in_specs=placed,
        out_specs=(
            P("dp", None),
            P("dp", None),
            P(None, None, "tensor"),
            P(None, "tensor"),
            P("tensor", None),
            P(),
            P(None, "tensor"),
            P("tensor"),
            P("tensor", None),
            P(),
            P(),
            P(),
            P(),
            P(),
        ),
        check_vma=False,
    )
```

```python
import functools

import jax
import jax.numpy as jnp
import numpy as np
from jax import lax
from jax.experimental import pallas as pl
from jax.experimental.pallas import tpu as pltpu
from jax.sharding import PartitionSpec as P

HEAD_DIM = 64
ROT_DIM = 16
EPS = 1e-05
F32 = jnp.float32
BF16 = jnp.bfloat16
MESH = pl.DeviceIdType.MESH

GROUP = 16
UNIT = 32
LAG = 2
SLOTS = 8
FIRST = 3
CHUNK = 256
FWD_PARTS = (1, 2, 2, 4)
BACK_PARTS = (2, 4, 4, 8)


def rotary_tables(length):
    places = np.arange(length, dtype=np.float64)
    rates = 10000.0 ** (-np.arange(0, ROT_DIM, 2, dtype=np.float64) / ROT_DIM)
    angles = places[:, None] * rates[None, :]
    cosine = np.ones((length, 2 * HEAD_DIM), np.float32)
    sine = np.zeros((length, 2 * HEAD_DIM), np.float32)
    for start in (0, 8, HEAD_DIM, HEAD_DIM + 8):
        cosine[:, start : start + 8] = np.cos(angles)
        sine[:, start : start + 8] = np.sin(angles)
    return cosine, sine


def nn(left, right):
    return lax.dot_general(
        left, right, (((1,), (0,)), ((), ())), preferred_element_type=F32
    )


def nt(left, right):
    return lax.dot_general(
        left, right, (((1,), (1,)), ((), ())), preferred_element_type=F32
    )


def remote(src, dst, send, recv, device):
    return pltpu.make_async_remote_copy(
        src_ref=src,
        dst_ref=dst,
        send_sem=send,
        recv_sem=recv,
        device_id=device,
        device_id_type=MESH,
    )


def aligned(value, multiple):
    return pl.multiple_of(value, multiple)


class Place:
    def __init__(self):
        index = lax.axis_index("dp")
        base = index - lax.rem(index, GROUP)
        self.core = lax.rem(index, 2)
        self.x = lax.rem(index // 2, 2)
        z = lax.rem(index // 4, 4)

        def at(line, pair, core):
            return {"dp": base + (line * 2 + pair) * 2 + core}

        self.middle = (z == 1) | (z == 2)
        self.end = jnp.logical_not(self.middle)
        self.half = z // 2
        self.to_core = at(z, self.x, 1 - self.core)
        self.to_x = at(z, 1 - self.x, self.core)
        self.to_middle = at(jnp.where(z == 0, 1, 2), self.x, self.core)
        self.to_end = at(jnp.where(z == 1, 0, 3), self.x, self.core)
        self.to_pair = at(jnp.where(z == 1, 2, 1), self.x, self.core)
        self.to_y = {"tensor": 1 - lax.axis_index("tensor")}

    def meet(self):
        barrier = pltpu.get_barrier_semaphore()

        def signal(device):
            pl.semaphore_signal(barrier, inc=1, device_id=device, device_id_type=MESH)

        signal(self.to_core)
        signal(self.to_x)
        signal(self.to_y)

        @pl.when(self.middle)
        def _():
            signal(self.to_end)
            signal(self.to_pair)
            pl.semaphore_wait(barrier, 5)

        @pl.when(self.end)
        def _():
            signal(self.to_middle)
            pl.semaphore_wait(barrier, 4)


def all_reduce_step(step, units, place, total, slots, send, recv, finish):
    quarter = UNIT // 4
    x, half = place.x, place.half
    slot_x, slot_ae, slot_be, slot_am, slot_bm, slot_bx, slot_af = slots

    def rows(unit, offset, count):
        return total.at[pl.ds(aligned(unit * UNIT + offset, 8), count)]

    def part_a(unit, which):
        return rows(unit, which * quarter, quarter)

    def part_b(unit, which):
        return rows(unit, 2 * quarter + which * quarter, quarter)

    def whole_b(unit):
        return rows(unit, 2 * quarter, 2 * quarter)

    def copy(kind, slot, src, dst, device):
        return remote(src, dst, send.at[kind, slot], recv.at[kind, slot], device)

    def stage(number, condition=None):
        unit = step - FIRST - (number - 1) * LAG
        active = (unit >= 0) & (unit < units)
        if condition is not None:
            active = active & condition

        def run(body):
            @pl.when(active)
            def _():
                body(unit, lax.rem(unit, SLOTS))

        return run

    def x_halves(u, s):
        return copy(0, s, part_a(u, 1 - x), slot_x.at[s], place.to_x)

    def a_to_middle(u, s):
        return copy(1, s, part_a(u, x), slot_ae.at[s], place.to_middle)

    def b_to_middle(u, s):
        return copy(2, s, whole_b(u), slot_be.at[s], place.to_middle)

    def a_exchange(u, s):
        return copy(3, s, part_a(u, x), slot_am.at[s], place.to_pair)

    def b_halves(u, s):
        return copy(4, s, part_b(u, 1 - half), slot_bm.at[s], place.to_pair)

    def b_exchange(u, s):
        return copy(5, s, part_b(u, half), slot_bx.at[s], place.to_x)

    def a_to_end(u, s):
        return copy(6, s, part_a(u, x), slot_af.at[s], place.to_end)

    def b_to_pair(u, s):
        return copy(7, s, part_b(u, half), part_b(u, half), place.to_pair)

    def b_to_end(u, s):
        return copy(8, s, whole_b(u), whole_b(u), place.to_end)

    def a_to_x(u, s):
        return copy(9, s, part_a(u, x), part_a(u, x), place.to_x)

    @stage(6, place.middle)
    def _(u, s):
        b_to_end(u, s).wait_send()

    @stage(6, place.end)
    def _(u, s):
        copy(8, s, whole_b(u), whole_b(u), place.to_middle).wait_recv()
        a_to_x(u, s).wait_send()

    @stage(6)
    def _(u, s):
        copy(9, s, part_a(u, 1 - x), part_a(u, 1 - x), place.to_x).wait_recv()
        finish(u)

    @stage(5, place.end)
    def _(u, s):
        copy(6, s, part_a(u, x), slot_af.at[s], place.to_middle).wait_recv()
        part_a(u, x)[...] = slot_af[s]
        a_to_x(u, s).start()

    @stage(5, place.middle)
    def _(u, s):
        copy(7, s, part_b(u, 1 - half), part_b(u, 1 - half), place.to_pair).wait_recv()
        b_to_end(u, s).start()
        a_to_end(u, s).wait_send()
        a_to_x(u, s).wait_send()
        b_to_pair(u, s).wait_send()

    @stage(3, place.end)
    def _(u, s):
        a_to_middle(u, s).wait_send()

    @stage(3, place.middle)
    def _(u, s):
        copy(1, s, part_a(u, x), slot_ae.at[s], place.to_end).wait_recv()
        b_halves(u, s).wait()
        part_a(u, x)[...] += slot_ae[s]
        a_exchange(u, s).start()
        part_b(u, half)[...] += slot_bm[s]
        b_exchange(u, s).start()

    @stage(4, place.middle)
    def _(u, s):
        a_exchange(u, s).wait()
        b_exchange(u, s).wait()
        part_a(u, x)[...] += slot_am[s]
        a_to_end(u, s).start()
        a_to_x(u, s).start()
        part_b(u, half)[...] += slot_bx[s]
        b_to_pair(u, s).start()

    @stage(2)
    def _(u, s):
        x_halves(u, s).wait()
        part_a(u, x)[...] += slot_x[s]

    @stage(2, place.end)
    def _(u, s):
        b_to_middle(u, s).wait_send()
        a_to_middle(u, s).start()

    @stage(2, place.middle)
    def _(u, s):
        copy(2, s, whole_b(u), slot_be.at[s], place.to_end).wait_recv()
        whole_b(u)[...] += slot_be[s]
        b_halves(u, s).start()

    @stage(1)
    def _(u, s):
        x_halves(u, s).start()

    @stage(1, place.end)
    def _(u, s):
        b_to_middle(u, s).start()


def rotated(values, cosine, sine, lane, direction):
    later = pltpu.roll(values, 2 * HEAD_DIM - 8, 1)
    earlier = pltpu.roll(values, 8, 1)
    turned = jnp.where(lane < 8, -direction * later, direction * earlier)
    return values * cosine + turned * sine


class Plan:
    def __init__(self, chunks, blocks, heads, dense_messages, qkv_messages):
        self.chunks, self.blocks = chunks, blocks
        tasks, uses = [], []
        self.full_use, self.mix_use, self.mix_first = {}, {}, {}

        def full(chunk):
            self.full_use[chunk] = len(uses)
            uses.append(chunk)
            tasks.extend(("full", 3 * chunk + part) for part in range(3))

        done = 2
        for chunk in range(done):
            full(chunk)
        self.floor = {chunk: 0 for chunk in range(done)}
        for block in range(blocks):
            tasks.append(("project", block))
            tasks.extend(("attend", block, part) for part in range(FWD_PARTS[block]))
            self.mix_use[block], self.mix_first[block] = len(uses), done
            uses.extend(range(done, chunks))
            tasks.append(("mix", block))
            if 0 < block < blocks - 1:
                self.floor[done] = block + 1
                full(done)
                done += 1
        for chunk in range(done, chunks):
            self.floor[chunk] = blocks
            full(chunk)
        tasks.append(("end_full", 0))
        tasks.extend(("dense", part) for part in range(dense_messages))
        tasks.append(("back_start", 0))
        for block in reversed(range(blocks)):
            tasks.extend(("back", block, part) for part in range(BACK_PARTS[block]))
            tasks.append(("rows", block))
        tasks.append(("transpose", 0))
        tasks.extend(("qkv", part) for part in range(qkv_messages))
        tasks.append(("small", 0))
        tasks.append(("small", 1))
        tasks.append(("small", 2))
        self.tasks, self.uses = tasks, uses
        self.collects = {}
        ready = {}
        for step, task in enumerate(tasks):
            new = []
            if task[0] == "full" and task[1] % 3 == 2:
                new = [2 * (task[1] // 3), 2 * (task[1] // 3) + 1]
            if task[0] == "dense":
                new = [2 * chunks + task[1]]
            if task[0] == "qkv":
                new = [2 * chunks + dense_messages + task[1]]
            for place, message in enumerate(new):
                at = step + 1 + place + (task[0] == "qkv")
                assert at not in self.collects
                self.collects[at] = message
                ready[message] = at
        per = 128 // UNIT
        for message, at in ready.items():
            assert at <= message * per + FIRST, (message, at, message * per + FIRST)

    def steps(self, name, *rest):
        return [
            (step, task[len(rest) + 1])
            for step, task in enumerate(self.tasks)
            if task[0] == name and task[1 : 1 + len(rest)] == rest
        ]


def pick(index, entries):
    entries = sorted(entries)
    runs = []
    for place, value in entries:
        if runs and place == runs[-1][1] + 1 and value == runs[-1][2] + place - runs[-1][0]:
            runs[-1][1] = place
        else:
            runs.append([place, place, value])
    found, result = False, 0
    for first, last, value in runs:
        here = (index >= first) & (index <= last)
        found = here | found
        result = jnp.where(here, value + index - first, result)
    return result, found


def layer_kernel(
    sizes,
    x_in,
    g_in,
    qkv_in,
    dense_in,
    fc1_in,
    fc2_in,
    vectors,
    fc1_bias,
    qkv_bias,
    cosine_in,
    sine_in,
    mixed_out,
    grad_out,
    fc1_out,
    fc2_out,
    dense_out,
    qkv_out,
    small_out,
    branch_other,
    norm_other,
    total,
    stage,
    core_in,
    slot_x,
    slot_ae,
    slot_be,
    slot_am,
    slot_bm,
    slot_bx,
    slot_af,
    x_ref,
    g_ref,
    ln_ref,
    ln_t,
    branch,
    norm,
    fc1_ref,
    fc2_ref,
    qkv_ref,
    dense_ref,
    q_ref,
    k_ref,
    v_ref,
    kv_t,
    o_t,
    do_ref,
    dq_t,
    dk_ref,
    dv_ref,
    cosine,
    sine,
    act_t,
    hg_ref,
    lse,
    fc1_bias_sum,
    qkv_bias_sum,
    small,
    small_y,
    small_core,
    send,
    recv,
    core_send,
    core_recv,
    load_sem,
    weight_sem,
    out_sem,
    y_send,
    y_recv,
    row_sem,
):
    tokens, width, local, hidden = sizes
    heads = local // HEAD_DIM
    chunks = hidden // CHUNK
    blocks = tokens // 256
    wide = width // 256
    place = Place()
    core = place.core
    fc_messages = 2 * chunks
    dense_messages = local // 256
    qkv_first = fc_messages + dense_messages
    qkv_messages = 3 * local // 256
    messages = qkv_first + qkv_messages
    per_message = 128 // UNIT
    units = messages * per_message + 1
    small_unit = units - 1
    plan = Plan(chunks, blocks, heads, dense_messages, qkv_messages)

    def load(src, dst, which):
        return pltpu.make_async_copy(src, dst, load_sem.at[which])

    def chunk_load(use):
        chunk, _ = pick(use, list(enumerate(plan.uses)))
        slot = lax.rem(use, 2)
        at = pl.ds(aligned(chunk * CHUNK, CHUNK), CHUNK)
        return (
            pltpu.make_async_copy(
                fc1_in.at[:, at], fc1_ref.at[slot], weight_sem.at[slot, 0]
            ),
            pltpu.make_async_copy(fc2_in.at[at], fc2_ref.at[slot], weight_sem.at[slot, 1]),
        )

    def take_chunk(use):
        for item in chunk_load(use):
            item.wait()

        @pl.when(use + 1 < len(plan.uses))
        def _():
            for item in chunk_load(use + 1):
                item.start()

        return lax.rem(use, 2)

    loads = [
        load(x_in, x_ref, 0),
        load(g_in, g_ref, 1),
        load(qkv_in, qkv_ref, 2),
        load(cosine_in, cosine, 3),
        load(sine_in, sine, 4),
        load(dense_in, dense_ref, 5),
    ]
    loads[0].start()
    for item in chunk_load(0):
        item.start()
    for item in loads[1:]:
        item.start()

    def row_block(index, size=256):
        return pl.ds(aligned(index * size, size), size)

    def normed_rows(rows):
        values = x_ref[rows, :].astype(F32)
        centered = values - jnp.mean(values, -1, keepdims=True)
        variance = jnp.mean(centered * centered, -1, keepdims=True)
        inverse = lax.rsqrt(variance + EPS)
        return centered * inverse, inverse

    def scaled_rows(rows, gain, offset):
        normed, _ = normed_rows(rows)
        return (normed * vectors[gain : gain + 1] + vectors[offset : offset + 1]).astype(BF16)


    def core_copy(message):
        slot = lax.rem(message, 4)
        return remote(
            stage.at[slot, pl.ds(aligned((1 - core) * 128, 128), 128)],
            core_in.at[slot],
            core_send.at[slot],
            core_recv.at[slot],
            place.to_core,
        )

    def collect(message):
        core_copy(message).wait()
        slot = lax.rem(message, 4)

        def body(index, carry):
            at = pl.ds(aligned(index * 32, 32), 32)
            own = stage[slot, pl.ds(aligned(core * 128 + index * 32, 32), 32)]
            total[pl.ds(aligned(message * 128 + index * 32, 32), 32)] = own + core_in[slot, at]
            return carry

        lax.fori_loop(0, 4, body, 0)


    def put(src, dst):
        pltpu.make_async_copy(src, dst, out_sem.at[0]).start()
        remote(src, dst, out_sem.at[1], out_sem.at[2], place.to_core).start()

    def finish(unit):
        message = unit // per_message
        at = core * 128 + lax.rem(unit, per_message) * UNIT
        rows = pl.ds(aligned(unit * UNIT, UNIT), UNIT)

        @pl.when((message < fc_messages) & (lax.rem(message, 2) == 0))
        def _():
            put(
                total.at[rows],
                fc2_out.at[pl.ds(aligned(message // 2 * CHUNK + at, UNIT), UNIT)],
            )

        @pl.when((message < fc_messages) & (lax.rem(message, 2) == 1))
        def _():
            columns = pl.ds(aligned(message // 2 * CHUNK, CHUNK), CHUNK)
            for part in range(wide):
                put(
                    total.at[rows, pl.ds(part * 256, 256)],
                    fc1_out.at[pl.ds(aligned(part * 256 + at, UNIT), UNIT), columns],
                )

        @pl.when((message >= fc_messages) & (message < qkv_first))
        def _():
            first = (message - fc_messages) * 256
            put(total.at[rows], dense_out.at[pl.ds(aligned(first + at, UNIT), UNIT)])

        @pl.when((message >= qkv_first) & (unit < small_unit))
        def _():
            which = message - qkv_first
            member = which // (local // 256)
            first = lax.rem(which, local // 256) * 256
            for part in range(width // local):
                put(
                    total.at[rows, pl.ds(part * local, local)],
                    qkv_out.at[member, pl.ds(aligned(part * local + first + at, UNIT), UNIT)],
                )

        @pl.when(unit == small_unit)
        def _():
            put(
                total.at[pl.ds(small_unit * UNIT, 8)],
                small_out.at[pl.ds(aligned(core * 8, 8), 8)],
            )


    def gate(rows, slot, offset):
        values = nn(ln_ref[rows, :], fc1_ref[slot]) + offset
        return values, 0.5 + 0.5 * lax.erf(values * 0.7071067811865476)

    def full_body(chunk, slot, part, floor):
        offset = fc1_bias[pl.ds(chunk, 1)]

        @pl.when(part == 0)
        def _():
            fc1_bias_sum[pl.ds(chunk, 1)] = jnp.zeros((1, CHUNK), F32)

        def body(step, bias_sum):
            index = part * (blocks // 2) + step
            rows = row_block(index)
            values, share = gate(rows, slot, offset)
            back = nt(g_ref[rows, :], fc2_ref[slot])
            act = (values * share).astype(BF16)
            slope = share + values * (jnp.exp(values * values * -0.5) * 0.3989422804014327)
            hg = (back * slope).astype(BF16)
            act_t[:, rows] = act.T
            hg_ref[rows, :] = hg
            norm[rows, :] += nt(hg, fc1_ref[slot])

            @pl.when(index >= floor)
            def _():
                branch[rows, :] += nn(act, fc2_ref[slot])

            return bias_sum + jnp.sum(hg.astype(F32), 0, keepdims=True)

        bias_sum = lax.fori_loop(0, blocks // 2, body, jnp.zeros((1, CHUNK), F32))
        fc1_bias_sum[pl.ds(chunk, 1)] += bias_sum

    def full_grads(chunk):
        message = 2 * chunk
        first, second = lax.rem(message, 4), lax.rem(message + 1, 4)

        def fc2_grad(index, carry):
            columns = row_block(index)
            stage[first, :, columns] = nn(act_t[...], g_ref[:, columns])
            return carry

        lax.fori_loop(0, wide, fc2_grad, 0)
        core_copy(message).start()

        def fc1_grad(index, carry):
            columns = row_block(index)
            stage[second, :, columns] = nn(ln_t[columns, :], hg_ref[...])
            return carry

        lax.fori_loop(0, wide, fc1_grad, 0)
        core_copy(message + 1).start()

    lane = lax.rem(lax.broadcasted_iota(jnp.int32, (256, 2 * HEAD_DIM), 1), HEAD_DIM)
    lane_head = lax.broadcasted_iota(jnp.int32, (256, 2 * HEAD_DIM), 1) // HEAD_DIM
    causal = lax.broadcasted_iota(jnp.int32, (256, 256), 0) <= lax.broadcasted_iota(
        jnp.int32, (256, 256), 1
    )

    def end_full():
        def body(index, sums):
            rows = row_block(index, 128)
            grad = norm[rows, :]
            norm[rows, :] = grad * vectors[2:3]
            dk_ref[rows, :] = jnp.zeros((128, local), F32)
            dv_ref[rows, :] = jnp.zeros((128, local), F32)
            return (
                sums[0] + jnp.sum(grad * normed_rows(rows)[0], 0, keepdims=True),
                sums[1] + jnp.sum(grad, 0, keepdims=True),
                sums[2] + jnp.sum(g_ref[rows, :].astype(F32), 0, keepdims=True),
            )

        zero = jnp.zeros((1, width), F32)
        sums = lax.fori_loop(0, tokens // 128, body, (zero, zero, zero))
        small[10:11] = sums[0]
        small[11:12] = sums[1]
        small[0:1] = sums[2]


    def project(block):
        rows = row_block(block)
        first = scaled_rows(rows, 0, 1)
        for member, target in enumerate((q_ref, k_ref, v_ref)):
            values = nn(first, qkv_ref[member]) + qkv_bias[member : member + 1].astype(F32)
            for pair in range(heads // 2):
                lanes = slice(pair * 128, pair * 128 + 128)
                part = values[:, lanes]
                if member < 2:
                    part = rotated(part, cosine[rows, :], sine[rows, :], lane, 1.0)
                if member == 0:
                    part = part * HEAD_DIM**-0.5
                target[rows, lanes] = part.astype(BF16)
            if member == 2:
                kv_t[:, rows] = values.astype(BF16).T

    def head_lanes(head):
        return pl.ds(aligned(head // 2 * 128, 128), 128)

    def one_head(values, head):
        return jnp.where(lane_head == lax.rem(head, 2), values, jnp.zeros_like(values))

    def attend(block, head):
        lanes = head_lanes(head)
        head_rows = pl.ds(aligned(head * HEAD_DIM, HEAD_DIM), HEAD_DIM)
        start = block * 256
        rows = slice(start, start + 256)
        query = one_head(q_ref[rows, lanes], head)
        near = nt(k_ref[rows, lanes], query)
        near = jnp.where(causal, near, -jnp.inf)
        peak = jnp.max(near, 0, keepdims=True)
        if block:
            far = nt(k_ref[0:start, lanes], query)
            peak = jnp.maximum(peak, jnp.max(far, 0, keepdims=True))
        near = jnp.exp(near - peak)
        weight = jnp.sum(near, 0, keepdims=True)
        result = nn(kv_t[head_rows, rows], near.astype(BF16))
        if block:
            far = jnp.exp(far - peak)
            weight = weight + jnp.sum(far, 0, keepdims=True)
            result = result + nn(kv_t[head_rows, 0:start], far.astype(BF16))
        o_t[head_rows, rows] = (result / weight).astype(BF16)
        lse[pl.ds(head, 1), rows] = peak + jnp.log(weight)

    def branch_copy(block):
        rows = row_block(block)
        return remote(
            branch.at[rows], branch_other.at[rows], y_send.at[block], y_recv.at[block], place.to_y
        )

    def norm_copy(block):
        rows, at = row_block(block), blocks + block
        return remote(norm.at[rows], norm_other.at[rows], y_send.at[at], y_recv.at[at], place.to_y)

    def mix(block):
        rows = row_block(block)
        first_use, _ = pick(block, list(plan.mix_use.items()))
        first_chunk, _ = pick(block, list(plan.mix_first.items()))

        def body(chunk, carry):
            slot = take_chunk(first_use + chunk - first_chunk)
            values, share = gate(rows, slot, fc1_bias[pl.ds(chunk, 1)])
            branch[rows, :] += nn((values * share).astype(BF16), fc2_ref[slot])
            return carry

        lax.fori_loop(first_chunk, chunks, body, 0)
        branch[rows, :] += nn(o_t[:, rows].T, dense_ref[...])
        branch_copy(block).start()

    def dense_grad(part):
        message = fc_messages + part
        slot = lax.rem(message, 4)

        def body(index, carry):
            columns = row_block(index)
            stage[slot, :, columns] = nn(o_t[row_block(part), :], g_ref[:, columns])
            return carry

        lax.fori_loop(0, wide, body, 0)
        core_copy(message).start()

    def back_start():
        def body(index, carry):
            rows = row_block(index)
            do_ref[rows, :] = nt(g_ref[rows, :], dense_ref[...]).astype(BF16)
            kv_t[:, rows] = k_ref[rows, :].T
            return carry

        lax.fori_loop(0, blocks, body, 0)
        for row in (8, 9):
            small[row : row + 1] = jnp.zeros((1, width), F32)
        qkv_bias_sum[...] = jnp.zeros_like(qkv_bias_sum)

    def attend_back(block, head):
        lanes = head_lanes(head)
        head_rows = pl.ds(aligned(head * HEAD_DIM, HEAD_DIM), HEAD_DIM)
        start = block * 256
        rows = slice(start, start + 256)
        query = one_head(q_ref[rows, lanes], head)
        grad = one_head(do_ref[rows, lanes], head)
        stat = lse[pl.ds(head, 1), rows]
        near = jnp.exp(jnp.where(causal, nt(k_ref[rows, lanes], query), -jnp.inf) - stat)
        near_back = nt(v_ref[rows, lanes], grad)
        centre = jnp.sum(near * near_back, 0, keepdims=True)
        if block:
            far = jnp.exp(nt(k_ref[0:start, lanes], query) - stat)
            far_back = nt(v_ref[0:start, lanes], grad)
            centre = centre + jnp.sum(far * far_back, 0, keepdims=True)
        dv_ref[rows, lanes] += nn(near.astype(BF16), grad)
        near = (near * (near_back - centre)).astype(BF16)
        dk_ref[rows, lanes] += nn(near, query)
        result = nn(kv_t[head_rows, rows], near)
        if block:
            dv_ref[0:start, lanes] += nn(far.astype(BF16), grad)
            far = (far * (far_back - centre)).astype(BF16)
            dk_ref[0:start, lanes] += nn(far, query)
            result = result + nn(kv_t[head_rows, 0:start], far)
        dq_t[head_rows, :] = result

    def end_rows(block):
        rows = row_block(block)
        for pair in range(heads // 2):
            lanes = slice(pair * 128, pair * 128 + 128)
            part = dq_t[lanes, :].T * HEAD_DIM**-0.5
            tables = cosine[rows, :], sine[rows, :], lane, -1.0
            q_ref[rows, lanes] = rotated(part, *tables).astype(BF16)
            k_ref[rows, lanes] = rotated(dk_ref[rows, lanes], *tables).astype(BF16)
        v_ref[rows, :] = dv_ref[rows, :].astype(BF16)
        grad = nt(q_ref[rows, :], qkv_ref[0])
        grad = grad + nt(k_ref[rows, :], qkv_ref[1])
        grad = grad + nt(v_ref[rows, :], qkv_ref[2])
        norm[rows, :] += grad * vectors[0:1]
        norm_copy(block).start()
        small[8:9] += jnp.sum(grad * normed_rows(rows)[0], 0, keepdims=True)
        small[9:10] += jnp.sum(grad, 0, keepdims=True)
        for member, ref in enumerate((q_ref, k_ref, v_ref)):
            qkv_bias_sum[member : member + 1] += jnp.sum(
                ref[rows, :].astype(F32), 0, keepdims=True
            )

    def transpose_first():
        def body(index, carry):
            rows = row_block(index, 128)
            ln_t[:, rows] = scaled_rows(rows, 0, 1).T
            return carry

        lax.fori_loop(0, tokens // 128, body, 0)

    def qkv_grad(which):
        message = qkv_first + which
        slot = lax.rem(message, 4)
        first = lax.rem(which, local // 256) * 256
        for member, target in enumerate((q_ref, k_ref, v_ref)):

            @pl.when(which // (local // 256) == member)
            def _(target=target):
                for part in range(width // local):
                    left = ln_t[pl.ds(aligned(part * local + first, 256), 256), :]
                    stage[slot, :, part * local : part * local + local] = nn(left, target[...])

        core_copy(message).start()


    def small_copy():
        at = 2 * blocks
        return remote(small.at[8:16], small_y, y_send.at[at], y_recv.at[at], place.to_y)

    def small_core_copy():
        at = 2 * blocks + 1
        return remote(
            small.at[pl.ds(aligned((1 - core) * 8, 8), 8)],
            small_core,
            y_send.at[at],
            y_recv.at[at],
            place.to_core,
        )

    def gather_small():
        small[12:16] = jnp.zeros((4, width), F32)
        small[5:8] = jnp.zeros((3, width), F32)
        for part in range(hidden // CHUNK):
            row, at = part * CHUNK // width, part * CHUNK % width
            small[1 + row : 2 + row, at : at + CHUNK] = fc1_bias_sum[part : part + 1]
        small[4:5] = jnp.zeros((1, width), F32)
        for member in range(3):
            row, at = member * local // width, member * local % width
            small[3 + row : 4 + row, at : at + local] = qkv_bias_sum[member : member + 1]
        small_copy().start()

    def small_cores():
        small_copy().wait()
        small[8:16] += small_y[...]
        small_core_copy().start()

    def end_small():
        small_core_copy().wait()
        total[pl.ds(small_unit * UNIT, UNIT)] = jnp.zeros((UNIT, width), F32)
        total[pl.ds(small_unit * UNIT, 8)] = (
            small[pl.ds(aligned(core * 8, 8), 8)] + small_core[...]
        )


    def other_rows(block, src, slot):
        return pltpu.make_async_copy(src.at[row_block(block)], stage.at[slot], row_sem.at[0])

    def mixed_copy(block):
        rows = row_block(block)
        return pltpu.make_async_copy(ln_ref.at[rows], mixed_out.at[rows], row_sem.at[1 + block])

    def grad_copy(block):
        rows = row_block(block)
        return pltpu.make_async_copy(
            ln_t.at[rows], grad_out.at[rows], row_sem.at[1 + blocks + block]
        )

    def end_mixed(block):
        branch_copy(block).wait()
        copy = other_rows(block, branch_other, 0)
        copy.start()
        copy.wait()

        def body(index, carry):
            at = pl.ds(aligned(index * 64, 64), 64)
            rows = pl.ds(aligned(block * 256 + index * 64, 64), 64)
            shares = branch[rows, :] + stage[0, at]
            ln_ref[rows, :] = (
                x_ref[rows, :].astype(F32) + shares + (vectors[4:5] + vectors[5:6])
            ).astype(BF16)
            return carry

        lax.fori_loop(0, 4, body, 0)
        mixed_copy(block).start()

    def end_grad(block):
        norm_copy(block).wait()
        copy = other_rows(block, norm_other, 1)
        copy.start()
        copy.wait()

        def body(index, carry):
            at = pl.ds(aligned(index * 64, 64), 64)
            rows = pl.ds(aligned(block * 256 + index * 64, 64), 64)
            normed, inverse = normed_rows(rows)
            scaled = norm[rows, :] + stage[1, at]
            mean = jnp.mean(scaled, -1, keepdims=True)
            slope = jnp.mean(scaled * normed, -1, keepdims=True)
            ln_t[rows, :] = (
                g_ref[rows, :].astype(F32) + inverse * (scaled - mean - normed * slope)
            ).astype(BF16)
            return carry

        lax.fori_loop(0, 4, body, 0)
        grad_copy(block).start()

    def clear(index, carry):
        rows = row_block(index, 128)
        branch[rows, :] = jnp.zeros((128, width), F32)
        norm[rows, :] = jnp.zeros((128, width), F32)
        low = scaled_rows(rows, 2, 3)
        ln_ref[rows, :] = low
        ln_t[:, rows] = low.T
        return carry

    loads[0].wait()
    lax.fori_loop(0, tokens // 128, clear, 0)
    for item in loads[1:]:
        item.wait()
    place.meet()

    steps = units + FIRST + 5 * LAG
    mixed_at = len(plan.tasks)
    grad_at = [steps - 4 * (1 + index) for index in range(blocks)][::-1]
    assert mixed_at + blocks <= grad_at[0]

    def step_body(step, carry):
        message, found = pick(step, list(plan.collects.items()))

        @pl.when(found)
        def _():
            collect(message)

        all_reduce_step(
            step,
            units,
            place,
            total,
            (slot_x, slot_ae, slot_be, slot_am, slot_bm, slot_bx, slot_af),
            send,
            recv,
            finish,
        )

        def task(body, name, *rest):
            value, found = pick(step, plan.steps(name, *rest))

            @pl.when(found)
            def _():
                body(value)

        def full(value):
            chunk, part = value // 3, lax.rem(value, 3)
            use, _ = pick(chunk, list(plan.full_use.items()))

            @pl.when(part == 0)
            def _():
                take_chunk(use)

            @pl.when(part < 2)
            def _():
                floor, _ = pick(chunk, list(plan.floor.items()))
                full_body(chunk, lax.rem(use, 2), part, floor)

            @pl.when(part == 2)
            def _():
                full_grads(chunk)

        task(full, "full")
        task(project, "project")
        for block in range(blocks):

            def some_heads(part, block=block):
                count = heads // FWD_PARTS[block]

                def body(index, carry):
                    attend(block, part * count + index)
                    return carry

                lax.fori_loop(0, count, body, 0)

            task(some_heads, "attend", block)
        task(mix, "mix")
        task(lambda value: end_full(), "end_full")
        task(dense_grad, "dense")
        task(lambda value: back_start(), "back_start")
        for block in range(blocks):

            def some_heads_back(part, block=block):
                count = heads // BACK_PARTS[block]

                def body(index, carry):
                    attend_back(block, part * count + index)
                    return carry

                lax.fori_loop(0, count, body, 0)

            task(some_heads_back, "back", block)
        task(end_rows, "rows")
        task(lambda value: transpose_first(), "transpose")
        task(qkv_grad, "qkv")
        for part, body in enumerate((gather_small, small_cores, end_small)):

            @pl.when(step == plan.steps("small")[part][0])
            def _(body=body):
                body()

        @pl.when((step >= mixed_at) & (step < mixed_at + blocks))
        def _():
            end_mixed(step - mixed_at)

        block, found = pick(step, [(at, blocks - 1 - index) for index, at in enumerate(grad_at)])

        @pl.when(found)
        def _():
            end_grad(block)

        return carry

    lax.fori_loop(0, steps, step_body, 0)

    done = total.at[pl.ds(0, small_unit * UNIT + 8)]
    pltpu.make_async_copy(done, done, out_sem.at[0]).wait()
    every = remote(done, done, out_sem.at[1], out_sem.at[2], place.to_core)
    every.wait_send()
    every.wait_recv()
    for block in range(blocks):
        mixed_copy(block).wait()
        grad_copy(block).wait()


def layer(tokens, cotangent, qkv_weight, dense_weight, fc1_weight, fc2_weight, vectors, fc1_bias, qkv_bias):
    rows, width = tokens.shape
    local, hidden = qkv_weight.shape[2], fc1_weight.shape[1]
    cosine, sine = (jnp.asarray(table) for table in rotary_tables(rows))
    hbm = pl.BlockSpec(memory_space=pl.ANY)
    vmem = pl.BlockSpec(memory_space=pltpu.VMEM)
    quarter = UNIT // 4
    chunks = hidden // CHUNK
    blocks = rows // 256
    unit_rows = (2 * chunks + local // 256 + 3 * local // 256) * 128 + UNIT
    dma = pltpu.SemaphoreType.DMA
    scratch = [
        pltpu.VMEM((unit_rows, width), F32),
        pltpu.VMEM((4, 256, width), F32),
        pltpu.VMEM((4, 128, width), F32),
        pltpu.VMEM((SLOTS, quarter, width), F32),
        pltpu.VMEM((SLOTS, quarter, width), F32),
        pltpu.VMEM((SLOTS, 2 * quarter, width), F32),
        pltpu.VMEM((SLOTS, quarter, width), F32),
        pltpu.VMEM((SLOTS, quarter, width), F32),
        pltpu.VMEM((SLOTS, quarter, width), F32),
        pltpu.VMEM((SLOTS, quarter, width), F32),
        pltpu.VMEM((rows, width), BF16),
        pltpu.VMEM((rows, width), BF16),
        pltpu.VMEM((rows, width), BF16),
        pltpu.VMEM((width, rows), BF16),
        pltpu.VMEM((rows, width), F32),
        pltpu.VMEM((rows, width), F32),
        pltpu.VMEM((2, width, CHUNK), BF16),
        pltpu.VMEM((2, CHUNK, width), BF16),
        pltpu.VMEM((3, width, local), BF16),
        pltpu.VMEM((local, width), BF16),
        pltpu.VMEM((rows, local), BF16),
        pltpu.VMEM((rows, local), BF16),
        pltpu.VMEM((rows, local), BF16),
        pltpu.VMEM((local, rows), BF16),
        pltpu.VMEM((local, rows), BF16),
        pltpu.VMEM((rows, local), BF16),
        pltpu.VMEM((local, 256), F32),
        pltpu.VMEM((rows, local), F32),
        pltpu.VMEM((rows, local), F32),
        pltpu.VMEM((rows, 2 * HEAD_DIM), F32),
        pltpu.VMEM((rows, 2 * HEAD_DIM), F32),
        pltpu.VMEM((CHUNK, rows), BF16),
        pltpu.VMEM((rows, CHUNK), BF16),
        pltpu.VMEM((local // HEAD_DIM, rows), F32),
        pltpu.VMEM((chunks, CHUNK), F32),
        pltpu.VMEM((3, local), F32),
        pltpu.VMEM((16, width), F32),
        pltpu.VMEM((8, width), F32),
        pltpu.VMEM((8, width), F32),
        dma((10, SLOTS)),
        dma((10, SLOTS)),
        dma((4,)),
        dma((4,)),
        dma((6,)),
        dma((2, 2)),
        dma((3,)),
        dma((2 * blocks + 2,)),
        dma((2 * blocks + 2,)),
        dma((1 + 2 * blocks,)),
    ]
    out = jax.ShapeDtypeStruct
    return pl.pallas_call(
        functools.partial(layer_kernel, (rows, width, local, hidden)),
        out_shape=[
            out((rows, width), BF16),
            out((rows, width), BF16),
            out((width, hidden), F32),
            out((hidden, width), F32),
            out((local, width), F32),
            out((3, width, local), F32),
            out((16, width), F32),
            out((rows, width), F32),
            out((rows, width), F32),
        ],
        in_specs=[hbm] * 6 + [vmem] * 3 + [hbm] * 2,
        out_specs=[hbm] * 9,
        scratch_shapes=scratch,
        compiler_params=pltpu.CompilerParams(
            collective_id=0, has_side_effects=True, vmem_limit_bytes=63 * 2**20
        ),
    )(
        tokens,
        cotangent,
        jnp.transpose(qkv_weight, (1, 0, 2)),
        dense_weight,
        fc1_weight,
        fc2_weight,
        vectors,
        fc1_bias,
        qkv_bias,
        cosine,
        sine,
    )


def per_device(
    groups,
    tokens,
    qkv_weight,
    qkv_bias,
    dense_weight,
    dense_bias,
    fc1_weight,
    fc1_bias,
    fc2_weight,
    fc2_bias,
    ln1_gain,
    ln1_bias,
    ln2_gain,
    ln2_bias,
    cotangent,
):
    width = tokens.shape[1]
    local, hidden = qkv_weight.shape[2], fc1_weight.shape[1]
    chunks = hidden // CHUNK
    vectors = jnp.concatenate([ln1_gain, ln1_bias, ln2_gain, ln2_bias, dense_bias, fc2_bias])
    mixed, input_grad, fc1_grad, fc2_grad, dense_grad, qkv_grad, small, _, _ = layer(
        tokens,
        cotangent,
        qkv_weight,
        dense_weight,
        fc1_weight,
        fc2_weight,
        vectors.astype(F32).reshape(6, width),
        fc1_bias.astype(F32).reshape(chunks, CHUNK),
        qkv_bias,
    )
    if groups is not None:
        fc1_grad, fc2_grad, dense_grad, qkv_grad, small = lax.psum(
            (fc1_grad, fc2_grad, dense_grad, qkv_grad, small), "dp", axis_index_groups=groups
        )
    flat = small.reshape(-1)
    bias_grad = small[0]
    return (
        mixed,
        input_grad,
        jnp.transpose(qkv_grad, (1, 0, 2)),
        flat[3 * width : 3 * width + 3 * local].reshape(3, local),
        dense_grad,
        bias_grad,
        fc1_grad,
        flat[width : width + hidden],
        fc2_grad,
        bias_grad,
        small[8],
        small[9],
        small[10],
        small[11],
    )


def solution(mesh):
    dp = mesh.shape["dp"]
    groups = None
    if dp > GROUP:
        groups = [[start + i for start in range(0, dp, GROUP)] for i in range(GROUP)]
    placed = (
        P("dp", None),
        P(None, None, "tensor"),
        P(None, "tensor"),
        P("tensor", None),
        P(),
        P(None, "tensor"),
        P("tensor"),
        P("tensor", None),
        P(),
        P(),
        P(),
        P(),
        P(),
        P("dp", None),
    )
    return jax.shard_map(
        functools.partial(per_device, groups),
        mesh=mesh,
        in_specs=placed,
        out_specs=(
            P("dp", None),
            P("dp", None),
            P(None, None, "tensor"),
            P(None, "tensor"),
            P("tensor", None),
            P(),
            P(None, "tensor"),
            P("tensor"),
            P("tensor", None),
            P(),
            P(),
            P(),
            P(),
            P(),
        ),
        check_vma=False,
    )
```

```python
import functools

import jax
import jax.numpy as jnp
import numpy as np
from jax import lax
from jax.experimental import pallas as pl
from jax.experimental.pallas import tpu as pltpu
from jax.sharding import PartitionSpec as P

HEAD_DIM = 64
ROT_DIM = 16
EPS = 1e-05
F32 = jnp.float32
BF16 = jnp.bfloat16
MESH = pl.DeviceIdType.MESH

GROUP = 16
UNIT = 32
LAG = 3
SLOTS = 12
WEIGHT_SLOTS = 3
EARLY = 2
CHUNK = 256
FWD_PARTS = (1, 2, 2, 4)
BACK_PARTS = (2, 4, 4, 4)
BACK_DOUBLE = (2, 3)


def rotary_tables(length):
    places = np.arange(length, dtype=np.float64)
    rates = 10000.0 ** (-np.arange(0, ROT_DIM, 2, dtype=np.float64) / ROT_DIM)
    angles = places[:, None] * rates[None, :]
    cosine = np.ones((length, 2 * HEAD_DIM), np.float32)
    sine = np.zeros((length, 2 * HEAD_DIM), np.float32)
    for start in (0, 8, HEAD_DIM, HEAD_DIM + 8):
        cosine[:, start : start + 8] = np.cos(angles)
        sine[:, start : start + 8] = np.sin(angles)
    return cosine, sine


def nn(left, right):
    return lax.dot_general(
        left, right, (((1,), (0,)), ((), ())), preferred_element_type=F32
    )


def nt(left, right):
    return lax.dot_general(
        left, right, (((1,), (1,)), ((), ())), preferred_element_type=F32
    )


def remote(src, dst, send, recv, device):
    return pltpu.make_async_remote_copy(
        src_ref=src,
        dst_ref=dst,
        send_sem=send,
        recv_sem=recv,
        device_id=device,
        device_id_type=MESH,
    )


def aligned(value, multiple):
    return pl.multiple_of(value, multiple)


class Place:
    def __init__(self):
        index = lax.axis_index("dp")
        base = index - lax.rem(index, GROUP)
        self.core = lax.rem(index, 2)
        self.x = lax.rem(index // 2, 2)
        z = lax.rem(index // 4, 4)

        def at(line, pair, core):
            return {"dp": base + (line * 2 + pair) * 2 + core}

        self.middle = (z == 1) | (z == 2)
        self.end = jnp.logical_not(self.middle)
        self.half = z // 2
        self.to_core = at(z, self.x, 1 - self.core)
        self.to_x = at(z, 1 - self.x, self.core)
        self.to_middle = at(jnp.where(z == 0, 1, 2), self.x, self.core)
        self.to_end = at(jnp.where(z == 1, 0, 3), self.x, self.core)
        self.to_pair = at(jnp.where(z == 1, 2, 1), self.x, self.core)
        self.to_y = {"tensor": 1 - lax.axis_index("tensor")}

    def meet(self):
        barrier = pltpu.get_barrier_semaphore()

        def signal(device):
            pl.semaphore_signal(barrier, inc=1, device_id=device, device_id_type=MESH)

        signal(self.to_core)
        signal(self.to_x)
        signal(self.to_y)

        @pl.when(self.middle)
        def _():
            signal(self.to_end)
            signal(self.to_pair)
            pl.semaphore_wait(barrier, 5)

        @pl.when(self.end)
        def _():
            signal(self.to_middle)
            pl.semaphore_wait(barrier, 4)


def all_reduce_step(step, units, place, total, slots, send, recv, finish):
    quarter = UNIT // 4
    x, half = place.x, place.half
    slot_x, slot_ae, slot_be, slot_am, slot_bm, slot_bx, slot_af = slots

    def rows(unit, offset, count):
        return total.at[pl.ds(aligned(unit * UNIT + offset, 8), count)]

    def part_a(unit, which):
        return rows(unit, which * quarter, quarter)

    def part_b(unit, which):
        return rows(unit, 2 * quarter + which * quarter, quarter)

    def whole_b(unit):
        return rows(unit, 2 * quarter, 2 * quarter)

    def copy(kind, slot, src, dst, device):
        return remote(src, dst, send.at[kind, slot], recv.at[kind, slot], device)

    def stage(number, condition=None):
        unit = step - (number - 1) * LAG
        active = (unit >= 0) & (unit < units)
        if condition is not None:
            active = active & condition

        def run(body):
            @pl.when(active)
            def _():
                body(unit, lax.rem(unit, SLOTS))

        return run

    def x_halves(u, s):
        return copy(0, s, part_a(u, 1 - x), slot_x.at[s], place.to_x)

    def a_to_middle(u, s):
        return copy(1, s, part_a(u, x), slot_ae.at[s], place.to_middle)

    def b_to_middle(u, s):
        return copy(2, s, whole_b(u), slot_be.at[s], place.to_middle)

    def a_exchange(u, s):
        return copy(3, s, part_a(u, x), slot_am.at[s], place.to_pair)

    def b_halves(u, s):
        return copy(4, s, part_b(u, 1 - half), slot_bm.at[s], place.to_pair)

    def b_exchange(u, s):
        return copy(5, s, part_b(u, half), slot_bx.at[s], place.to_x)

    def a_to_end(u, s):
        return copy(6, s, part_a(u, x), slot_af.at[s], place.to_end)

    def b_to_pair(u, s):
        return copy(7, s, part_b(u, half), part_b(u, half), place.to_pair)

    def b_to_end(u, s):
        return copy(8, s, whole_b(u), whole_b(u), place.to_end)

    def a_to_x(u, s):
        return copy(9, s, part_a(u, x), part_a(u, x), place.to_x)

    @stage(6, place.middle)
    def _(u, s):
        b_to_end(u, s).wait_send()

    @stage(6, place.end)
    def _(u, s):
        copy(8, s, whole_b(u), whole_b(u), place.to_middle).wait_recv()
        a_to_x(u, s).wait_send()

    @stage(6)
    def _(u, s):
        copy(9, s, part_a(u, 1 - x), part_a(u, 1 - x), place.to_x).wait_recv()
        finish(u)

    @stage(5, place.end)
    def _(u, s):
        copy(6, s, part_a(u, x), slot_af.at[s], place.to_middle).wait_recv()
        part_a(u, x)[...] = slot_af[s]
        a_to_x(u, s).start()

    @stage(5, place.middle)
    def _(u, s):
        copy(7, s, part_b(u, 1 - half), part_b(u, 1 - half), place.to_pair).wait_recv()
        b_to_end(u, s).start()
        a_to_end(u, s).wait_send()
        a_to_x(u, s).wait_send()
        b_to_pair(u, s).wait_send()

    @stage(3, place.end)
    def _(u, s):
        a_to_middle(u, s).wait_send()

    @stage(3, place.middle)
    def _(u, s):
        copy(1, s, part_a(u, x), slot_ae.at[s], place.to_end).wait_recv()
        b_halves(u, s).wait()
        part_a(u, x)[...] += slot_ae[s]
        a_exchange(u, s).start()
        part_b(u, half)[...] += slot_bm[s]
        b_exchange(u, s).start()

    @stage(4, place.middle)
    def _(u, s):
        a_exchange(u, s).wait()
        b_exchange(u, s).wait()
        part_a(u, x)[...] += slot_am[s]
        a_to_end(u, s).start()
        a_to_x(u, s).start()
        part_b(u, half)[...] += slot_bx[s]
        b_to_pair(u, s).start()

    @stage(2)
    def _(u, s):
        x_halves(u, s).wait()
        part_a(u, x)[...] += slot_x[s]

    @stage(2, place.end)
    def _(u, s):
        b_to_middle(u, s).wait_send()
        a_to_middle(u, s).start()

    @stage(2, place.middle)
    def _(u, s):
        copy(2, s, whole_b(u), slot_be.at[s], place.to_end).wait_recv()
        whole_b(u)[...] += slot_be[s]
        b_halves(u, s).start()

    @stage(1)
    def _(u, s):
        x_halves(u, s).start()

    @stage(1, place.end)
    def _(u, s):
        b_to_middle(u, s).start()


def rotated(values, cosine, sine, lane, direction):
    later = pltpu.roll(values, 2 * HEAD_DIM - 8, 1)
    earlier = pltpu.roll(values, 8, 1)
    turned = jnp.where(lane < 8, -direction * later, direction * earlier)
    return values * cosine + turned * sine


class Plan:
    def __init__(self, chunks, blocks, heads, dense_messages, qkv_messages):
        self.chunks, self.blocks = chunks, blocks
        tasks, uses = [], []
        self.use = {}

        def full(chunk):
            self.use["full", chunk] = len(uses)
            uses.append(chunk)
            tasks.extend(("full", 3 * chunk + part) for part in range(3))

        def attention(block):
            tasks.append(("project", block))
            tasks.extend(("attend", block, part) for part in range(FWD_PARTS[block]))
            tasks.append(("mix", block))

        tasks.append(("first", 0))
        self.use["first", 0] = 0
        uses.extend(range(chunks))
        attention(0)
        for chunk in range(EARLY):
            full(chunk)
        for chunk in range(EARLY, chunks):
            self.use["ahead", chunk] = len(uses)
            uses.append(chunk)
            tasks.append(("ahead", chunk))
        done = EARLY
        for block in range(1, blocks):
            attention(block)
            if block < blocks - 1:
                full(done)
                done += 1
        for chunk in range(done, chunks):
            full(chunk)
        tasks.append(("back_start", 0))
        for block in reversed(range(blocks)):
            tasks.extend(("back", block, part) for part in range(BACK_PARTS[block]))
            tasks.append(("rows", block))
            if block == blocks - 1:
                tasks.extend(("dense", part) for part in range(dense_messages))
        tasks.append(("transpose", 0))
        tasks.extend(("qkv", part) for part in range(qkv_messages))
        tasks.append(("small", 0))
        tasks.append(("small", 1))
        tasks.append(("small", 2))
        self.tasks, self.uses = tasks, uses
        self.collects = {}
        ready = {}
        for step, task in enumerate(tasks):
            new = []
            if task[0] == "full" and task[1] % 3 == 2:
                new = [2 * (task[1] // 3), 2 * (task[1] // 3) + 1]
            if task[0] == "dense":
                new = [2 * chunks + task[1]]
            if task[0] == "qkv":
                new = [2 * chunks + dense_messages + task[1]]
            for place, message in enumerate(new):
                at = step + 1 + place + (task[0] == "qkv")
                assert at not in self.collects
                self.collects[at] = message
                ready[message] = at
        self.start = min(ready.values())
        self.moves, self.total = {}, 0
        for step in range(self.start, len(tasks)):
            task = tasks[step]
            long = task[0] == "back" and task[1] in BACK_DOUBLE
            here = 0
            while here < 2 if long else here < 1:
                if step < ready.get(self.total * UNIT // 128, 0):
                    break
                here += 1
                self.total += 1
            self.moves[step] = here

    def steps(self, name, *rest):
        return [
            (step, task[len(rest) + 1])
            for step, task in enumerate(self.tasks)
            if task[0] == name and task[1 : 1 + len(rest)] == rest
        ]


def pick(index, entries):
    entries = sorted(entries)
    runs = []
    for place, value in entries:
        if runs and place == runs[-1][1] + 1 and value == runs[-1][2] + place - runs[-1][0]:
            runs[-1][1] = place
        else:
            runs.append([place, place, value])
    found, result = False, 0
    for first, last, value in runs:
        here = (index >= first) & (index <= last)
        found = here | found
        result = jnp.where(here, value + index - first, result)
    return result, found


def layer_kernel(
    sizes,
    x_in,
    g_in,
    qkv_in,
    dense_in,
    fc1_in,
    fc2_in,
    vectors,
    fc1_bias,
    qkv_bias,
    cosine_in,
    sine_in,
    mixed_out,
    grad_out,
    fc1_out,
    fc2_out,
    dense_out,
    qkv_out,
    small_out,
    branch_other,
    norm_other,
    total,
    stage,
    core_in,
    slot_x,
    slot_ae,
    slot_be,
    slot_am,
    slot_bm,
    slot_bx,
    slot_af,
    x_ref,
    g_ref,
    ln_ref,
    ln_t,
    branch,
    norm,
    fc1_ref,
    fc2_ref,
    qkv_ref,
    dense_ref,
    q_ref,
    k_ref,
    v_ref,
    kv_t,
    o_t,
    do_ref,
    dq_t,
    dk_ref,
    dv_ref,
    cosine,
    sine,
    act_t,
    hg_ref,
    lse,
    fc1_bias_sum,
    qkv_bias_sum,
    small,
    small_y,
    small_core,
    send,
    recv,
    core_send,
    core_recv,
    load_sem,
    weight_sem,
    out_sem,
    y_send,
    y_recv,
    row_sem,
):
    tokens, width, local, hidden = sizes
    heads = local // HEAD_DIM
    chunks = hidden // CHUNK
    blocks = tokens // 256
    wide = width // 256
    place = Place()
    core = place.core
    fc_messages = 2 * chunks
    dense_messages = local // 256
    qkv_first = fc_messages + dense_messages
    qkv_messages = 3 * local // 256
    messages = qkv_first + qkv_messages
    per_message = 128 // UNIT
    units = messages * per_message + 1
    small_unit = units - 1
    plan = Plan(chunks, blocks, heads, dense_messages, qkv_messages)

    def load(src, dst, which):
        return pltpu.make_async_copy(src, dst, load_sem.at[which])

    def chunk_load(use):
        chunk, _ = pick(use, list(enumerate(plan.uses)))
        slot = lax.rem(use, WEIGHT_SLOTS)
        at = pl.ds(aligned(chunk * CHUNK, CHUNK), CHUNK)
        return (
            pltpu.make_async_copy(
                fc1_in.at[:, at], fc1_ref.at[slot], weight_sem.at[slot, 0]
            ),
            pltpu.make_async_copy(fc2_in.at[at], fc2_ref.at[slot], weight_sem.at[slot, 1]),
        )

    def take_chunk(use):
        for item in chunk_load(use):
            item.wait()

        ahead = use + WEIGHT_SLOTS - 1

        @pl.when(ahead < len(plan.uses))
        def _():
            for item in chunk_load(ahead):
                item.start()

        return lax.rem(use, WEIGHT_SLOTS)

    loads = [
        load(x_in, x_ref, 0),
        load(g_in, g_ref, 1),
        load(qkv_in, qkv_ref, 2),
        load(cosine_in, cosine, 3),
        load(sine_in, sine, 4),
        load(dense_in, dense_ref, 5),
    ]
    loads[0].start()
    for item in chunk_load(0):
        item.start()
    loads[1].start()
    for use in range(1, WEIGHT_SLOTS - 1):
        for item in chunk_load(use):
            item.start()
    for item in loads[2:]:
        item.start()

    def row_block(index, size=256):
        return pl.ds(aligned(index * size, size), size)

    def normed_rows(rows):
        values = x_ref[rows, :].astype(F32)
        centered = values - jnp.mean(values, -1, keepdims=True)
        variance = jnp.mean(centered * centered, -1, keepdims=True)
        inverse = lax.rsqrt(variance + EPS)
        return centered * inverse, inverse

    def scaled_rows(rows, gain, offset):
        normed, _ = normed_rows(rows)
        return (normed * vectors[gain : gain + 1] + vectors[offset : offset + 1]).astype(BF16)


    def core_copy(message):
        slot = lax.rem(message, 4)
        return remote(
            stage.at[slot, pl.ds(aligned((1 - core) * 128, 128), 128)],
            core_in.at[slot],
            core_send.at[slot],
            core_recv.at[slot],
            place.to_core,
        )

    def collect(message):
        core_copy(message).wait()
        slot = lax.rem(message, 4)

        def body(index, carry):
            at = pl.ds(aligned(index * 32, 32), 32)
            own = stage[slot, pl.ds(aligned(core * 128 + index * 32, 32), 32)]
            total[pl.ds(aligned(message * 128 + index * 32, 32), 32)] = own + core_in[slot, at]
            return carry

        lax.fori_loop(0, 4, body, 0)


    def put(src, dst):
        pltpu.make_async_copy(src, dst, out_sem.at[0]).start()
        remote(src, dst, out_sem.at[1], out_sem.at[2], place.to_core).start()

    def finish(unit):
        message = unit // per_message
        at = core * 128 + lax.rem(unit, per_message) * UNIT
        rows = pl.ds(aligned(unit * UNIT, UNIT), UNIT)

        @pl.when((message < fc_messages) & (lax.rem(message, 2) == 0))
        def _():
            put(
                total.at[rows],
                fc2_out.at[pl.ds(aligned(message // 2 * CHUNK + at, UNIT), UNIT)],
            )

        @pl.when((message < fc_messages) & (lax.rem(message, 2) == 1))
        def _():
            columns = pl.ds(aligned(message // 2 * CHUNK, CHUNK), CHUNK)
            for part in range(wide):
                put(
                    total.at[rows, pl.ds(part * 256, 256)],
                    fc1_out.at[pl.ds(aligned(part * 256 + at, UNIT), UNIT), columns],
                )

        @pl.when((message >= fc_messages) & (message < qkv_first))
        def _():
            first = (message - fc_messages) * 256
            put(total.at[rows], dense_out.at[pl.ds(aligned(first + at, UNIT), UNIT)])

        @pl.when((message >= qkv_first) & (unit < small_unit))
        def _():
            which = message - qkv_first
            member = which // (local // 256)
            first = lax.rem(which, local // 256) * 256
            for part in range(width // local):
                put(
                    total.at[rows, pl.ds(part * local, local)],
                    qkv_out.at[member, pl.ds(aligned(part * local + first + at, UNIT), UNIT)],
                )

        @pl.when(unit == small_unit)
        def _():
            put(
                total.at[pl.ds(small_unit * UNIT, 8)],
                small_out.at[pl.ds(aligned(core * 8, 8), 8)],
            )


    def gate(rows, slot, offset):
        values = nn(ln_ref[rows, :], fc1_ref[slot]) + offset
        return values, 0.5 + 0.5 * lax.erf(values * 0.7071067811865476)

    def full_body(chunk, slot, part):
        offset = fc1_bias[pl.ds(chunk, 1)]

        @pl.when(part == 0)
        def _():
            fc1_bias_sum[pl.ds(chunk, 1)] = jnp.zeros((1, CHUNK), F32)

        rows = row_block(part, tokens // 2)
        values, share = gate(rows, slot, offset)
        back = nt(g_ref[rows, :], fc2_ref[slot])
        act = (values * share).astype(BF16)
        slope = share + values * (jnp.exp(values * values * -0.5) * 0.3989422804014327)
        hg = (back * slope).astype(BF16)
        act_t[:, rows] = act.T
        hg_ref[rows, :] = hg
        norm[rows, :] += nt(hg, fc1_ref[slot])

        @pl.when((chunk < EARLY) & (part == 0))
        def _():
            branch[256 : tokens // 2, :] += nn(act[256:], fc2_ref[slot])

        @pl.when((chunk < EARLY) & (part == 1))
        def _():
            branch[tokens // 2 :, :] += nn(act, fc2_ref[slot])

        fc1_bias_sum[pl.ds(chunk, 1)] += jnp.sum(hg.astype(F32), 0, keepdims=True)

    def full_grads(chunk):
        message = 2 * chunk
        first, second = lax.rem(message, 4), lax.rem(message + 1, 4)

        stage[first] = nn(act_t[...], g_ref[...])
        core_copy(message).start()
        result = nn(ln_t[...], hg_ref[...])
        for index in range(wide):
            stage[second, :, index * 256 : index * 256 + 256] = result[
                index * 256 : index * 256 + 256
            ]
        core_copy(message + 1).start()

    lane = lax.rem(lax.broadcasted_iota(jnp.int32, (256, 2 * HEAD_DIM), 1), HEAD_DIM)
    lane_head = lax.broadcasted_iota(jnp.int32, (256, 2 * HEAD_DIM), 1) // HEAD_DIM
    causal = lax.broadcasted_iota(jnp.int32, (256, 512), 0) <= lax.rem(
        lax.broadcasted_iota(jnp.int32, (256, 512), 1), 256
    )


    def project(block):
        rows = row_block(block)
        first = scaled_rows(rows, 0, 1)
        for member, target in enumerate((q_ref, k_ref, v_ref)):
            values = nn(first, qkv_ref[member]) + qkv_bias[member : member + 1].astype(F32)
            for pair in range(heads // 2):
                lanes = slice(pair * 128, pair * 128 + 128)
                part = values[:, lanes]
                if member < 2:
                    part = rotated(part, cosine[rows, :], sine[rows, :], lane, 1.0)
                if member == 0:
                    part = part * HEAD_DIM**-0.5
                target[rows, lanes] = part.astype(BF16)
            if member == 2:
                kv_t[:, rows] = values.astype(BF16).T

    def both_heads(values):
        zero = jnp.zeros_like(values)
        return jnp.concatenate(
            [jnp.where(lane_head == 0, values, zero), jnp.where(lane_head == 1, values, zero)], 0
        )

    def own_heads(result):
        return jnp.concatenate([result[:HEAD_DIM, :256], result[HEAD_DIM:, 256:]], 0)

    def attend(block, pair):
        lanes = pl.ds(aligned(pair * 128, 128), 128)
        start = block * 256
        rows = slice(start, start + 256)
        query = both_heads(q_ref[rows, lanes])
        near = jnp.where(causal, nt(k_ref[rows, lanes], query), -jnp.inf)
        peak = jnp.max(near, 0, keepdims=True)
        if block:
            far = nt(k_ref[0:start, lanes], query)
            peak = jnp.maximum(peak, jnp.max(far, 0, keepdims=True))
        near = jnp.exp(near - peak)
        weight = jnp.sum(near, 0, keepdims=True)
        result = nn(kv_t[lanes, rows], near.astype(BF16))
        if block:
            far = jnp.exp(far - peak)
            weight = weight + jnp.sum(far, 0, keepdims=True)
            result = result + nn(kv_t[lanes, 0:start], far.astype(BF16))
        o_t[lanes, rows] = own_heads(result / weight).astype(BF16)
        lse[block, pl.ds(pair, 1)] = peak + jnp.log(weight)

    def branch_copy(block):
        rows = row_block(block)
        return remote(
            branch.at[rows], branch_other.at[rows], y_send.at[block], y_recv.at[block], place.to_y
        )

    def norm_copy(block):
        rows, at = row_block(block), blocks + block
        return remote(norm.at[rows], norm_other.at[rows], y_send.at[at], y_recv.at[at], place.to_y)

    def use_of(kind, chunk):
        return pick(chunk, [(at, use) for (name, at), use in plan.use.items() if name == kind])[0]

    def branch_share(rows, slot, chunk):
        values, share = gate(rows, slot, fc1_bias[pl.ds(chunk, 1)])
        branch[rows, :] += nn((values * share).astype(BF16), fc2_ref[slot])

    def first_block():
        def body(chunk, carry):
            branch_share(slice(0, 256), take_chunk(chunk), chunk)
            return carry

        lax.fori_loop(0, chunks, body, 0)

    def ahead(chunk):
        slot = take_chunk(use_of("ahead", chunk))
        branch_share(slice(256, tokens // 2), slot, chunk)
        branch_share(slice(tokens // 2, tokens), slot, chunk)

    def mix(block):
        rows = row_block(block)
        branch[rows, :] += nn(o_t[:, rows].T, dense_ref[...])
        branch_copy(block).start()

    def dense_grad(part):
        message = fc_messages + part
        slot = lax.rem(message, 4)

        stage[slot] = nn(o_t[row_block(part), :], g_ref[...])
        core_copy(message).start()

    def back_start():
        def body(index, carry):
            rows = row_block(index)
            do_ref[rows, :] = nt(g_ref[rows, :], dense_ref[...]).astype(BF16)
            kv_t[:, rows] = k_ref[rows, :].T
            return carry

        lax.fori_loop(0, blocks, body, 0)
        for row in range(8, 12):
            small[row : row + 1] = jnp.zeros((1, width), F32)
        qkv_bias_sum[...] = jnp.zeros_like(qkv_bias_sum)

    def attend_back(block, pair):
        lanes = pl.ds(aligned(pair * 128, 128), 128)
        start = block * 256
        rows = slice(start, start + 256)
        query = both_heads(q_ref[rows, lanes])
        grad = both_heads(do_ref[rows, lanes])
        stat = lse[block, pl.ds(pair, 1)]
        near = jnp.exp(jnp.where(causal, nt(k_ref[rows, lanes], query), -jnp.inf) - stat)
        near_back = nt(v_ref[rows, lanes], grad)
        centre = jnp.sum(near * near_back, 0, keepdims=True)
        if block:
            far = jnp.exp(nt(k_ref[0:start, lanes], query) - stat)
            far_back = nt(v_ref[0:start, lanes], grad)
            centre = centre + jnp.sum(far * far_back, 0, keepdims=True)

        def add(ref, here, value):
            ref[here, lanes] = value if block == blocks - 1 else ref[here, lanes] + value

        add(dv_ref, rows, nn(near.astype(BF16), grad))
        near = (near * (near_back - centre)).astype(BF16)
        add(dk_ref, rows, nn(near, query))
        result = nn(kv_t[lanes, rows], near)
        if block:
            far_rows = slice(0, start)
            add(dv_ref, far_rows, nn(far.astype(BF16), grad))
            far = (far * (far_back - centre)).astype(BF16)
            add(dk_ref, far_rows, nn(far, query))
            result = result + nn(kv_t[lanes, 0:start], far)
        dq_t[lanes, :] = own_heads(result)

    def end_rows(block):
        rows = row_block(block)
        for pair in range(heads // 2):
            lanes = slice(pair * 128, pair * 128 + 128)
            part = dq_t[lanes, :].T * HEAD_DIM**-0.5
            tables = cosine[rows, :], sine[rows, :], lane, -1.0
            q_ref[rows, lanes] = rotated(part, *tables).astype(BF16)
            k_ref[rows, lanes] = rotated(dk_ref[rows, lanes], *tables).astype(BF16)
        v_ref[rows, :] = dv_ref[rows, :].astype(BF16)
        grad = nt(q_ref[rows, :], qkv_ref[0])
        grad = grad + nt(k_ref[rows, :], qkv_ref[1])
        grad = grad + nt(v_ref[rows, :], qkv_ref[2])
        second = norm[rows, :]
        norm[rows, :] = second * vectors[2:3] + grad * vectors[0:1]
        norm_copy(block).start()
        normed, _ = normed_rows(rows)
        small[8:9] += jnp.sum(grad * normed, 0, keepdims=True)
        small[9:10] += jnp.sum(grad, 0, keepdims=True)
        small[10:11] += jnp.sum(second * normed, 0, keepdims=True)
        small[11:12] += jnp.sum(second, 0, keepdims=True)
        for member, ref in enumerate((q_ref, k_ref, v_ref)):
            qkv_bias_sum[member : member + 1] += jnp.sum(
                ref[rows, :].astype(F32), 0, keepdims=True
            )

    def transpose_first():
        def body(index, carry):
            rows = row_block(index, 128)
            ln_t[:, rows] = scaled_rows(rows, 0, 1).T
            return carry + jnp.sum(g_ref[rows, :].astype(F32), 0, keepdims=True)

        small[0:1] = lax.fori_loop(0, tokens // 128, body, jnp.zeros((1, width), F32))

    def qkv_grad(which):
        message = qkv_first + which
        slot = lax.rem(message, 4)
        first = lax.rem(which, local // 256) * 256
        for member, target in enumerate((q_ref, k_ref, v_ref)):

            @pl.when(which // (local // 256) == member)
            def _(target=target):
                for part in range(width // local):
                    left = ln_t[pl.ds(aligned(part * local + first, 256), 256), :]
                    stage[slot, :, part * local : part * local + local] = nn(left, target[...])

        core_copy(message).start()


    def small_copy():
        at = 2 * blocks
        return remote(small.at[8:16], small_y, y_send.at[at], y_recv.at[at], place.to_y)

    def small_core_copy():
        at = 2 * blocks + 1
        return remote(
            small.at[pl.ds(aligned((1 - core) * 8, 8), 8)],
            small_core,
            y_send.at[at],
            y_recv.at[at],
            place.to_core,
        )

    def gather_small():
        small[12:16] = jnp.zeros((4, width), F32)
        small[5:8] = jnp.zeros((3, width), F32)
        for part in range(hidden // CHUNK):
            row, at = part * CHUNK // width, part * CHUNK % width
            small[1 + row : 2 + row, at : at + CHUNK] = fc1_bias_sum[part : part + 1]
        small[4:5] = jnp.zeros((1, width), F32)
        for member in range(3):
            row, at = member * local // width, member * local % width
            small[3 + row : 4 + row, at : at + local] = qkv_bias_sum[member : member + 1]
        small_copy().start()

    def small_cores():
        small_copy().wait()
        small[8:16] += small_y[...]
        small_core_copy().start()

    def end_small():
        small_core_copy().wait()
        total[pl.ds(small_unit * UNIT, UNIT)] = jnp.zeros((UNIT, width), F32)
        total[pl.ds(small_unit * UNIT, 8)] = (
            small[pl.ds(aligned(core * 8, 8), 8)] + small_core[...]
        )


    def other_rows(block, src, slot):
        return pltpu.make_async_copy(src.at[row_block(block)], stage.at[slot], row_sem.at[0])

    def mixed_copy(block):
        rows = row_block(block)
        return pltpu.make_async_copy(ln_ref.at[rows], mixed_out.at[rows], row_sem.at[1 + block])

    def grad_copy(block):
        rows = row_block(block)
        return pltpu.make_async_copy(
            ln_t.at[rows], grad_out.at[rows], row_sem.at[1 + blocks + block]
        )

    def end_mixed(block):
        branch_copy(block).wait()
        copy = other_rows(block, branch_other, 0)
        copy.start()
        copy.wait()

        def body(index, carry):
            at = pl.ds(aligned(index * 64, 64), 64)
            rows = pl.ds(aligned(block * 256 + index * 64, 64), 64)
            shares = branch[rows, :] + stage[0, at]
            ln_ref[rows, :] = (
                x_ref[rows, :].astype(F32) + shares + (vectors[4:5] + vectors[5:6])
            ).astype(BF16)
            return carry

        lax.fori_loop(0, 4, body, 0)
        mixed_copy(block).start()

    def end_grad(block):
        norm_copy(block).wait()
        copy = other_rows(block, norm_other, 1)
        copy.start()
        copy.wait()

        def body(index, carry):
            at = pl.ds(aligned(index * 64, 64), 64)
            rows = pl.ds(aligned(block * 256 + index * 64, 64), 64)
            normed, inverse = normed_rows(rows)
            scaled = norm[rows, :] + stage[1, at]
            mean = jnp.mean(scaled, -1, keepdims=True)
            slope = jnp.mean(scaled * normed, -1, keepdims=True)
            ln_t[rows, :] = (
                g_ref[rows, :].astype(F32) + inverse * (scaled - mean - normed * slope)
            ).astype(BF16)
            return carry

        lax.fori_loop(0, 4, body, 0)
        grad_copy(block).start()

    def clear(index, carry):
        rows = row_block(index, 128)
        branch[rows, :] = jnp.zeros((128, width), F32)
        norm[rows, :] = jnp.zeros((128, width), F32)
        low = scaled_rows(rows, 2, 3)
        ln_ref[rows, :] = low
        ln_t[:, rows] = low.T
        return carry

    loads[0].wait()
    lax.fori_loop(0, tokens // 128, clear, 0)
    for item in loads[1:]:
        item.wait()
    place.meet()

    steps = len(plan.tasks) + units + 5 * LAG - plan.total
    mixed_at = len(plan.tasks)
    grad_at = [steps - 4 * (1 + index) for index in range(blocks)][::-1]


    def step_body(step, moved):
        message, found = pick(step, list(plan.collects.items()))

        @pl.when(found)
        def _():
            collect(message)

        moves = jnp.where(step < plan.start, 0, 1)
        for count in (0, 2):
            _, here = pick(step, [(at, 0) for at, moved in plan.moves.items() if moved == count])
            moves = jnp.where(here, count, moves)

        def move(index, carry):
            all_reduce_step(
                moved + index,
                units,
                place,
                total,
                (slot_x, slot_ae, slot_be, slot_am, slot_bm, slot_bx, slot_af),
                send,
                recv,
                finish,
            )
            return carry

        lax.fori_loop(0, moves, move, 0)

        def task(body, name, *rest):
            value, found = pick(step, plan.steps(name, *rest))

            @pl.when(found)
            def _():
                body(value)

        def full(value):
            chunk, part = value // 3, lax.rem(value, 3)
            use = use_of("full", chunk)

            @pl.when(part == 0)
            def _():
                take_chunk(use)

            @pl.when(part < 2)
            def _():
                full_body(chunk, lax.rem(use, WEIGHT_SLOTS), part)

            @pl.when(part == 2)
            def _():
                full_grads(chunk)

        task(full, "full")
        task(project, "project")
        for block in range(blocks):

            def some_heads(part, block=block):
                count = heads // 2 // FWD_PARTS[block]

                def body(index, carry):
                    attend(block, part * count + index)
                    return carry

                lax.fori_loop(0, count, body, 0)

            task(some_heads, "attend", block)
        task(lambda value: first_block(), "first")
        task(ahead, "ahead")
        task(mix, "mix")
        task(dense_grad, "dense")
        task(lambda value: back_start(), "back_start")
        for block in range(blocks):

            def some_heads_back(part, block=block):
                count = heads // 2 // BACK_PARTS[block]

                def body(index, carry):
                    attend_back(block, part * count + index)
                    return carry

                lax.fori_loop(0, count, body, 0)

            task(some_heads_back, "back", block)
        task(end_rows, "rows")
        task(lambda value: transpose_first(), "transpose")
        task(qkv_grad, "qkv")
        for part, body in enumerate((gather_small, small_cores, end_small)):

            @pl.when(step == plan.steps("small")[part][0])
            def _(body=body):
                body()

        @pl.when((step >= mixed_at) & (step < mixed_at + blocks))
        def _():
            end_mixed(step - mixed_at)

        block, found = pick(step, [(at, blocks - 1 - index) for index, at in enumerate(grad_at)])

        @pl.when(found)
        def _():
            end_grad(block)

        return moved + moves

    lax.fori_loop(0, steps, step_body, 0)

    done = total.at[pl.ds(0, small_unit * UNIT + 8)]
    pltpu.make_async_copy(done, done, out_sem.at[0]).wait()
    every = remote(done, done, out_sem.at[1], out_sem.at[2], place.to_core)
    every.wait_send()
    every.wait_recv()
    for block in range(blocks):
        mixed_copy(block).wait()
        grad_copy(block).wait()


def layer(tokens, cotangent, qkv_weight, dense_weight, fc1_weight, fc2_weight, vectors, fc1_bias, qkv_bias):
    rows, width = tokens.shape
    local, hidden = qkv_weight.shape[2], fc1_weight.shape[1]
    cosine, sine = (jnp.asarray(table) for table in rotary_tables(rows))
    hbm = pl.BlockSpec(memory_space=pl.ANY)
    vmem = pl.BlockSpec(memory_space=pltpu.VMEM)
    quarter = UNIT // 4
    chunks = hidden // CHUNK
    blocks = rows // 256
    unit_rows = (2 * chunks + local // 256 + 3 * local // 256) * 128 + UNIT
    dma = pltpu.SemaphoreType.DMA
    scratch = [
        pltpu.VMEM((unit_rows, width), F32),
        pltpu.VMEM((4, 256, width), F32),
        pltpu.VMEM((4, 128, width), F32),
        pltpu.VMEM((SLOTS, quarter, width), F32),
        pltpu.VMEM((SLOTS, quarter, width), F32),
        pltpu.VMEM((SLOTS, 2 * quarter, width), F32),
        pltpu.VMEM((SLOTS, quarter, width), F32),
        pltpu.VMEM((SLOTS, quarter, width), F32),
        pltpu.VMEM((SLOTS, quarter, width), F32),
        pltpu.VMEM((SLOTS, quarter, width), F32),
        pltpu.VMEM((rows, width), BF16),
        pltpu.VMEM((rows, width), BF16),
        pltpu.VMEM((rows, width), BF16),
        pltpu.VMEM((width, rows), BF16),
        pltpu.VMEM((rows, width), F32),
        pltpu.VMEM((rows, width), F32),
        pltpu.VMEM((WEIGHT_SLOTS, width, CHUNK), BF16),
        pltpu.VMEM((WEIGHT_SLOTS, CHUNK, width), BF16),
        pltpu.VMEM((3, width, local), BF16),
        pltpu.VMEM((local, width), BF16),
        pltpu.VMEM((rows, local), BF16),
        pltpu.VMEM((rows, local), BF16),
        pltpu.VMEM((rows, local), BF16),
        pltpu.VMEM((local, rows), BF16),
        pltpu.VMEM((local, rows), BF16),
        pltpu.VMEM((rows, local), BF16),
        pltpu.VMEM((local, 256), F32),
        pltpu.VMEM((rows, local), F32),
        pltpu.VMEM((rows, local), F32),
        pltpu.VMEM((rows, 2 * HEAD_DIM), F32),
        pltpu.VMEM((rows, 2 * HEAD_DIM), F32),
        pltpu.VMEM((CHUNK, rows), BF16),
        pltpu.VMEM((rows, CHUNK), BF16),
        pltpu.VMEM((blocks, local // 128, 512), F32),
        pltpu.VMEM((chunks, CHUNK), F32),
        pltpu.VMEM((3, local), F32),
        pltpu.VMEM((16, width), F32),
        pltpu.VMEM((8, width), F32),
        pltpu.VMEM((8, width), F32),
        dma((10, SLOTS)),
        dma((10, SLOTS)),
        dma((4,)),
        dma((4,)),
        dma((6,)),
        dma((WEIGHT_SLOTS, 2)),
        dma((3,)),
        dma((2 * blocks + 2,)),
        dma((2 * blocks + 2,)),
        dma((1 + 2 * blocks,)),
    ]
    out = jax.ShapeDtypeStruct
    return pl.pallas_call(
        functools.partial(layer_kernel, (rows, width, local, hidden)),
        out_shape=[
            out((rows, width), BF16),
            out((rows, width), BF16),
            out((width, hidden), F32),
            out((hidden, width), F32),
            out((local, width), F32),
            out((3, width, local), F32),
            out((16, width), F32),
            out((rows, width), F32),
            out((rows, width), F32),
        ],
        in_specs=[hbm] * 6 + [vmem] * 3 + [hbm] * 2,
        out_specs=[hbm] * 9,
        scratch_shapes=scratch,
        compiler_params=pltpu.CompilerParams(
            collective_id=0, has_side_effects=True, vmem_limit_bytes=63 * 2**20
        ),
    )(
        tokens,
        cotangent,
        jnp.transpose(qkv_weight, (1, 0, 2)),
        dense_weight,
        fc1_weight,
        fc2_weight,
        vectors,
        fc1_bias,
        qkv_bias,
        cosine,
        sine,
    )


def per_device(
    groups,
    tokens,
    qkv_weight,
    qkv_bias,
    dense_weight,
    dense_bias,
    fc1_weight,
    fc1_bias,
    fc2_weight,
    fc2_bias,
    ln1_gain,
    ln1_bias,
    ln2_gain,
    ln2_bias,
    cotangent,
):
    width = tokens.shape[1]
    local, hidden = qkv_weight.shape[2], fc1_weight.shape[1]
    chunks = hidden // CHUNK
    vectors = jnp.concatenate([ln1_gain, ln1_bias, ln2_gain, ln2_bias, dense_bias, fc2_bias])
    mixed, input_grad, fc1_grad, fc2_grad, dense_grad, qkv_grad, small, _, _ = layer(
        tokens,
        cotangent,
        qkv_weight,
        dense_weight,
        fc1_weight,
        fc2_weight,
        vectors.astype(F32).reshape(6, width),
        fc1_bias.astype(F32).reshape(chunks, CHUNK),
        qkv_bias,
    )
    if groups is not None:
        fc1_grad, fc2_grad, dense_grad, qkv_grad, small = lax.psum(
            (fc1_grad, fc2_grad, dense_grad, qkv_grad, small), "dp", axis_index_groups=groups
        )
    flat = small.reshape(-1)
    bias_grad = small[0]
    return (
        mixed,
        input_grad,
        jnp.transpose(qkv_grad, (1, 0, 2)),
        flat[3 * width : 3 * width + 3 * local].reshape(3, local),
        dense_grad,
        bias_grad,
        fc1_grad,
        flat[width : width + hidden],
        fc2_grad,
        bias_grad,
        small[8],
        small[9],
        small[10],
        small[11],
    )


def solution(mesh):
    dp = mesh.shape["dp"]
    groups = None
    if dp > GROUP:
        groups = [[start + i for start in range(0, dp, GROUP)] for i in range(GROUP)]
    placed = (
        P("dp", None),
        P(None, None, "tensor"),
        P(None, "tensor"),
        P("tensor", None),
        P(),
        P(None, "tensor"),
        P("tensor"),
        P("tensor", None),
        P(),
        P(),
        P(),
        P(),
        P(),
        P("dp", None),
    )
    return jax.shard_map(
        functools.partial(per_device, groups),
        mesh=mesh,
        in_specs=placed,
        out_specs=(
            P("dp", None),
            P("dp", None),
            P(None, None, "tensor"),
            P(None, "tensor"),
            P("tensor", None),
            P(),
            P(None, "tensor"),
            P("tensor"),
            P("tensor", None),
            P(),
            P(),
            P(),
            P(),
            P(),
        ),
        check_vma=False,
    )
```

```python
import functools

import jax
import jax.numpy as jnp
import numpy as np
from jax import lax
from jax.experimental import pallas as pl
from jax.experimental.pallas import tpu as pltpu
from jax.sharding import PartitionSpec as P

HEAD_DIM = 64
ROT_DIM = 16
EPS = 1e-05
F32 = jnp.float32
BF16 = jnp.bfloat16
MESH = pl.DeviceIdType.MESH

GROUP = 16
UNIT = 32
LAG = 3
SLOTS = 12
WEIGHT_SLOTS = 3
EARLY = 2
CHUNK = 256
FWD_PARTS = (1, 2, 2, 4)
BACK_PARTS = (2, 4, 4, 4)
BACK_DOUBLE = (2, 3)


def rotary_tables(length):
    places = np.arange(length, dtype=np.float64)
    rates = 10000.0 ** (-np.arange(0, ROT_DIM, 2, dtype=np.float64) / ROT_DIM)
    angles = places[:, None] * rates[None, :]
    cosine = np.ones((length, 2 * HEAD_DIM), np.float32)
    sine = np.zeros((length, 2 * HEAD_DIM), np.float32)
    for start in (0, 8, HEAD_DIM, HEAD_DIM + 8):
        cosine[:, start : start + 8] = np.cos(angles)
        sine[:, start : start + 8] = np.sin(angles)
    return cosine, sine


def nn(left, right):
    return lax.dot_general(
        left, right, (((1,), (0,)), ((), ())), preferred_element_type=F32
    )


def nt(left, right):
    return lax.dot_general(
        left, right, (((1,), (1,)), ((), ())), preferred_element_type=F32
    )


def remote(src, dst, send, recv, device):
    return pltpu.make_async_remote_copy(
        src_ref=src,
        dst_ref=dst,
        send_sem=send,
        recv_sem=recv,
        device_id=device,
        device_id_type=MESH,
    )


def aligned(value, multiple):
    return pl.multiple_of(value, multiple)


class Place:
    def __init__(self):
        index = lax.axis_index("dp")
        base = index - lax.rem(index, GROUP)
        self.core = lax.rem(index, 2)
        self.x = lax.rem(index // 2, 2)
        z = lax.rem(index // 4, 4)

        def at(line, pair, core):
            return {"dp": base + (line * 2 + pair) * 2 + core}

        self.middle = (z == 1) | (z == 2)
        self.end = jnp.logical_not(self.middle)
        self.half = z // 2
        self.to_core = at(z, self.x, 1 - self.core)
        self.to_x = at(z, 1 - self.x, self.core)
        self.to_middle = at(jnp.where(z == 0, 1, 2), self.x, self.core)
        self.to_end = at(jnp.where(z == 1, 0, 3), self.x, self.core)
        self.to_pair = at(jnp.where(z == 1, 2, 1), self.x, self.core)
        self.to_y = {"tensor": 1 - lax.axis_index("tensor")}

    def meet(self):
        barrier = pltpu.get_barrier_semaphore()

        def signal(device):
            pl.semaphore_signal(barrier, inc=1, device_id=device, device_id_type=MESH)

        signal(self.to_core)
        signal(self.to_x)
        signal(self.to_y)

        @pl.when(self.middle)
        def _():
            signal(self.to_end)
            signal(self.to_pair)
            pl.semaphore_wait(barrier, 5)

        @pl.when(self.end)
        def _():
            signal(self.to_middle)
            pl.semaphore_wait(barrier, 4)


def all_reduce_step(step, units, place, total, slots, send, recv, finish):
    quarter = UNIT // 4
    x, half = place.x, place.half
    slot_x, slot_ae, slot_be, slot_am, slot_bm, slot_bx, slot_af = slots

    def rows(unit, offset, count):
        return total.at[pl.ds(aligned(unit * UNIT + offset, 8), count)]

    def part_a(unit, which):
        return rows(unit, which * quarter, quarter)

    def part_b(unit, which):
        return rows(unit, 2 * quarter + which * quarter, quarter)

    def whole_b(unit):
        return rows(unit, 2 * quarter, 2 * quarter)

    def copy(kind, slot, src, dst, device):
        return remote(src, dst, send.at[kind, slot], recv.at[kind, slot], device)

    def stage(number, condition=None):
        unit = step - (number - 1) * LAG
        active = (unit >= 0) & (unit < units)
        if condition is not None:
            active = active & condition

        def run(body):
            @pl.when(active)
            def _():
                body(unit, lax.rem(unit, SLOTS))

        return run

    def x_halves(u, s):
        return copy(0, s, part_a(u, 1 - x), slot_x.at[s], place.to_x)

    def a_to_middle(u, s):
        return copy(1, s, part_a(u, x), slot_ae.at[s], place.to_middle)

    def b_to_middle(u, s):
        return copy(2, s, whole_b(u), slot_be.at[s], place.to_middle)

    def a_exchange(u, s):
        return copy(3, s, part_a(u, x), slot_am.at[s], place.to_pair)

    def b_halves(u, s):
        return copy(4, s, part_b(u, 1 - half), slot_bm.at[s], place.to_pair)

    def b_exchange(u, s):
        return copy(5, s, part_b(u, half), slot_bx.at[s], place.to_x)

    def a_to_end(u, s):
        return copy(6, s, part_a(u, x), slot_af.at[s], place.to_end)

    def b_to_pair(u, s):
        return copy(7, s, part_b(u, half), part_b(u, half), place.to_pair)

    def b_to_end(u, s):
        return copy(8, s, whole_b(u), whole_b(u), place.to_end)

    def a_to_x(u, s):
        return copy(9, s, part_a(u, x), part_a(u, x), place.to_x)

    @stage(6, place.middle)
    def _(u, s):
        b_to_end(u, s).wait_send()

    @stage(6, place.end)
    def _(u, s):
        copy(8, s, whole_b(u), whole_b(u), place.to_middle).wait_recv()
        a_to_x(u, s).wait_send()

    @stage(6)
    def _(u, s):
        copy(9, s, part_a(u, 1 - x), part_a(u, 1 - x), place.to_x).wait_recv()
        finish(u)

    @stage(5, place.end)
    def _(u, s):
        copy(6, s, part_a(u, x), slot_af.at[s], place.to_middle).wait_recv()
        part_a(u, x)[...] = slot_af[s]
        a_to_x(u, s).start()

    @stage(5, place.middle)
    def _(u, s):
        copy(7, s, part_b(u, 1 - half), part_b(u, 1 - half), place.to_pair).wait_recv()
        b_to_end(u, s).start()
        a_to_end(u, s).wait_send()
        a_to_x(u, s).wait_send()
        b_to_pair(u, s).wait_send()

    @stage(3, place.end)
    def _(u, s):
        a_to_middle(u, s).wait_send()

    @stage(3, place.middle)
    def _(u, s):
        copy(1, s, part_a(u, x), slot_ae.at[s], place.to_end).wait_recv()
        b_halves(u, s).wait()
        part_a(u, x)[...] += slot_ae[s]
        a_exchange(u, s).start()
        part_b(u, half)[...] += slot_bm[s]
        b_exchange(u, s).start()

    @stage(4, place.middle)
    def _(u, s):
        a_exchange(u, s).wait()
        b_exchange(u, s).wait()
        part_a(u, x)[...] += slot_am[s]
        a_to_end(u, s).start()
        a_to_x(u, s).start()
        part_b(u, half)[...] += slot_bx[s]
        b_to_pair(u, s).start()

    @stage(2)
    def _(u, s):
        x_halves(u, s).wait()
        part_a(u, x)[...] += slot_x[s]

    @stage(2, place.end)
    def _(u, s):
        b_to_middle(u, s).wait_send()
        a_to_middle(u, s).start()

    @stage(2, place.middle)
    def _(u, s):
        copy(2, s, whole_b(u), slot_be.at[s], place.to_end).wait_recv()
        whole_b(u)[...] += slot_be[s]
        b_halves(u, s).start()

    @stage(1)
    def _(u, s):
        x_halves(u, s).start()

    @stage(1, place.end)
    def _(u, s):
        b_to_middle(u, s).start()


def rotated(values, cosine, sine, lane, direction):
    later = pltpu.roll(values, 2 * HEAD_DIM - 8, 1)
    earlier = pltpu.roll(values, 8, 1)
    turned = jnp.where(lane < 8, -direction * later, direction * earlier)
    return values * cosine + turned * sine


class Plan:
    def __init__(self, chunks, blocks, heads, dense_messages, qkv_messages):
        self.chunks, self.blocks = chunks, blocks
        tasks, uses = [], []
        self.use = {}

        def full(chunk):
            self.use["full", chunk] = len(uses)
            uses.append(chunk)
            tasks.extend(("full", 3 * chunk + part) for part in range(3))

        def attention(block):
            tasks.append(("project", block))
            tasks.extend(("attend", block, part) for part in range(FWD_PARTS[block]))
            tasks.append(("mix", block))

        tasks.append(("first", 0))
        self.use["first", 0] = 0
        uses.extend(range(chunks))
        attention(0)
        for chunk in range(EARLY):
            full(chunk)
        for chunk in range(EARLY, chunks):
            self.use["ahead", chunk] = len(uses)
            uses.append(chunk)
            tasks.append(("ahead", chunk))
        done = EARLY
        for block in range(1, blocks):
            attention(block)
            if block < blocks - 1:
                full(done)
                done += 1
        for chunk in range(done, chunks):
            full(chunk)
        tasks.append(("back_start", 0))
        for block in reversed(range(blocks)):
            tasks.extend(("back", block, part) for part in range(BACK_PARTS[block]))
            tasks.append(("rows", block))
            if block == blocks - 1:
                tasks.extend(("dense", part) for part in range(dense_messages))
        tasks.append(("transpose", 0))
        tasks.extend(("qkv", part) for part in range(qkv_messages))
        tasks.append(("small", 0))
        tasks.append(("small", 1))
        tasks.append(("small", 2))
        self.tasks, self.uses = tasks, uses
        self.collects = {}
        ready = {}
        for step, task in enumerate(tasks):
            new = []
            if task[0] == "full" and task[1] % 3 == 2:
                new = [2 * (task[1] // 3), 2 * (task[1] // 3) + 1]
            if task[0] == "dense":
                new = [2 * chunks + task[1]]
            if task[0] == "qkv":
                new = [2 * chunks + dense_messages + task[1]]
            for place, message in enumerate(new):
                at = step + 1 + place + (task[0] == "qkv")
                assert at not in self.collects
                self.collects[at] = message
                ready[message] = at
        self.start = min(ready.values())
        self.moves, self.total = {}, 0
        for step in range(self.start, len(tasks)):
            task = tasks[step]
            long = task[0] == "back" and task[1] in BACK_DOUBLE
            here = 0
            while here < 2 if long else here < 1:
                if step < ready.get(self.total * UNIT // 128, 0):
                    break
                here += 1
                self.total += 1
            self.moves[step] = here

    def steps(self, name, *rest):
        return [
            (step, task[len(rest) + 1])
            for step, task in enumerate(self.tasks)
            if task[0] == name and task[1 : 1 + len(rest)] == rest
        ]


def pick(index, entries):
    entries = sorted(entries)
    runs = []
    for place, value in entries:
        if runs and place == runs[-1][1] + 1 and value == runs[-1][2] + place - runs[-1][0]:
            runs[-1][1] = place
        else:
            runs.append([place, place, value])
    found, result = False, 0
    for first, last, value in runs:
        here = (index >= first) & (index <= last)
        found = here | found
        result = jnp.where(here, value + index - first, result)
    return result, found


def layer_kernel(
    sizes,
    x_in,
    g_in,
    qkv_in,
    dense_in,
    fc1_in,
    fc2_in,
    vectors,
    qkv_bias,
    cosine_in,
    sine_in,
    mixed_out,
    grad_out,
    fc1_out,
    fc2_out,
    dense_out,
    qkv_out,
    small_out,
    branch_other,
    norm_other,
    total,
    stage,
    core_in,
    slot_x,
    slot_ae,
    slot_be,
    slot_am,
    slot_bm,
    slot_bx,
    slot_af,
    x_ref,
    g_ref,
    ln_ref,
    ln_t,
    branch,
    norm,
    fc1_ref,
    fc2_ref,
    qkv_ref,
    dense_ref,
    q_ref,
    k_ref,
    v_ref,
    kv_t,
    o_t,
    do_ref,
    dq_t,
    dk_ref,
    dv_ref,
    cosine,
    sine,
    act_t,
    hg_ref,
    lse,
    fc1_bias_sum,
    qkv_bias_sum,
    small,
    small_y,
    small_core,
    send,
    recv,
    core_send,
    core_recv,
    load_sem,
    weight_sem,
    out_sem,
    y_send,
    y_recv,
    row_sem,
):
    tokens, width, local, hidden = sizes
    heads = local // HEAD_DIM
    chunks = hidden // CHUNK
    blocks = tokens // 256
    wide = width // 256
    place = Place()
    core = place.core
    fc_messages = 2 * chunks
    dense_messages = local // 256
    qkv_first = fc_messages + dense_messages
    qkv_messages = 3 * local // 256
    messages = qkv_first + qkv_messages
    per_message = 128 // UNIT
    units = messages * per_message + 1
    small_unit = units - 1
    plan = Plan(chunks, blocks, heads, dense_messages, qkv_messages)

    def load(src, dst, which):
        return pltpu.make_async_copy(src, dst, load_sem.at[which])

    def chunk_load(use):
        chunk, _ = pick(use, list(enumerate(plan.uses)))
        slot = lax.rem(use, WEIGHT_SLOTS)
        at = pl.ds(aligned(chunk * CHUNK, CHUNK), CHUNK)
        return (
            pltpu.make_async_copy(
                fc1_in.at[:, at], fc1_ref.at[slot], weight_sem.at[slot, 0]
            ),
            pltpu.make_async_copy(fc2_in.at[at], fc2_ref.at[slot], weight_sem.at[slot, 1]),
        )

    def take_chunk(use):
        for item in chunk_load(use):
            item.wait()

        ahead = use + WEIGHT_SLOTS - 1

        @pl.when(ahead < len(plan.uses))
        def _():
            for item in chunk_load(ahead):
                item.start()

        return lax.rem(use, WEIGHT_SLOTS)

    loads = [
        load(x_in, x_ref, 0),
        load(g_in, g_ref, 1),
        load(qkv_in, qkv_ref, 2),
        load(cosine_in, cosine, 3),
        load(sine_in, sine, 4),
        load(dense_in, dense_ref, 5),
    ]
    loads[0].start()
    for item in chunk_load(0):
        item.start()
    loads[1].start()
    for use in range(1, WEIGHT_SLOTS - 1):
        for item in chunk_load(use):
            item.start()
    for item in loads[2:]:
        item.start()

    def row_block(index, size=256):
        return pl.ds(aligned(index * size, size), size)

    def normed_rows(rows):
        values = x_ref[rows, :].astype(F32)
        centered = values - jnp.mean(values, -1, keepdims=True)
        variance = jnp.mean(centered * centered, -1, keepdims=True)
        inverse = lax.rsqrt(variance + EPS)
        return centered * inverse, inverse

    def scaled_rows(rows, gain, offset):
        normed, _ = normed_rows(rows)
        return (normed * vectors[gain : gain + 1] + vectors[offset : offset + 1]).astype(BF16)


    def core_copy(message):
        slot = lax.rem(message, 4)
        return remote(
            stage.at[slot, pl.ds(aligned((1 - core) * 128, 128), 128)],
            core_in.at[slot],
            core_send.at[slot],
            core_recv.at[slot],
            place.to_core,
        )

    def collect(message):
        core_copy(message).wait()
        slot = lax.rem(message, 4)

        def body(index, carry):
            at = pl.ds(aligned(index * 32, 32), 32)
            own = stage[slot, pl.ds(aligned(core * 128 + index * 32, 32), 32)]
            total[pl.ds(aligned(message * 128 + index * 32, 32), 32)] = own + core_in[slot, at]
            return carry

        lax.fori_loop(0, 4, body, 0)


    def put(src, dst):
        pltpu.make_async_copy(src, dst, out_sem.at[0]).start()
        remote(src, dst, out_sem.at[1], out_sem.at[2], place.to_core).start()

    def finish(unit):
        message = unit // per_message
        at = core * 128 + lax.rem(unit, per_message) * UNIT
        rows = pl.ds(aligned(unit * UNIT, UNIT), UNIT)

        @pl.when((message < fc_messages) & (lax.rem(message, 2) == 0))
        def _():
            put(
                total.at[rows],
                fc2_out.at[pl.ds(aligned(message // 2 * CHUNK + at, UNIT), UNIT)],
            )

        @pl.when((message < fc_messages) & (lax.rem(message, 2) == 1))
        def _():
            columns = pl.ds(aligned(message // 2 * CHUNK, CHUNK), CHUNK)
            for part in range(wide):
                put(
                    total.at[rows, pl.ds(part * 256, 256)],
                    fc1_out.at[pl.ds(aligned(part * 256 + at, UNIT), UNIT), columns],
                )

        @pl.when((message >= fc_messages) & (message < qkv_first))
        def _():
            first = (message - fc_messages) * 256
            put(total.at[rows], dense_out.at[pl.ds(aligned(first + at, UNIT), UNIT)])

        @pl.when((message >= qkv_first) & (unit < small_unit))
        def _():
            which = message - qkv_first
            member = which // (local // 256)
            first = lax.rem(which, local // 256) * 256
            for part in range(width // local):
                put(
                    total.at[rows, pl.ds(part * local, local)],
                    qkv_out.at[member, pl.ds(aligned(part * local + first + at, UNIT), UNIT)],
                )

        @pl.when(unit == small_unit)
        def _():
            put(
                total.at[pl.ds(small_unit * UNIT, 8)],
                small_out.at[pl.ds(aligned(core * 8, 8), 8)],
            )


    def fc1_offset(chunk):
        per = width // CHUNK
        return vectors[
            pl.ds(6 + chunk // per, 1), pl.ds(aligned(lax.rem(chunk, per) * CHUNK, CHUNK), CHUNK)
        ]

    def gate(rows, slot, offset):
        values = nn(ln_ref[rows, :], fc1_ref[slot]) + offset
        return values, 0.5 + 0.5 * lax.erf(values * 0.7071067811865476)

    def full_body(chunk, slot, part):
        offset = fc1_offset(chunk)

        @pl.when(part == 0)
        def _():
            fc1_bias_sum[pl.ds(chunk, 1)] = jnp.zeros((1, CHUNK), F32)

        rows = row_block(part, tokens // 2)
        values, share = gate(rows, slot, offset)
        back = nt(g_ref[rows, :], fc2_ref[slot])
        act = (values * share).astype(BF16)
        slope = share + values * (jnp.exp(values * values * -0.5) * 0.3989422804014327)
        hg = (back * slope).astype(BF16)
        act_t[:, rows] = act.T
        hg_ref[rows, :] = hg
        norm[rows, :] += nt(hg, fc1_ref[slot])

        @pl.when((chunk < EARLY) & (part == 0))
        def _():
            branch[256 : tokens // 2, :] += nn(act[256:], fc2_ref[slot])

        @pl.when((chunk < EARLY) & (part == 1))
        def _():
            branch[tokens // 2 :, :] += nn(act, fc2_ref[slot])

        fc1_bias_sum[pl.ds(chunk, 1)] += jnp.sum(hg.astype(F32), 0, keepdims=True)

    def full_grads(chunk):
        message = 2 * chunk
        first, second = lax.rem(message, 4), lax.rem(message + 1, 4)

        stage[first] = nn(act_t[...], g_ref[...])
        core_copy(message).start()
        result = nn(ln_t[...], hg_ref[...])
        for index in range(wide):
            stage[second, :, index * 256 : index * 256 + 256] = result[
                index * 256 : index * 256 + 256
            ]
        core_copy(message + 1).start()

    lane = lax.rem(lax.broadcasted_iota(jnp.int32, (256, 2 * HEAD_DIM), 1), HEAD_DIM)
    lane_head = lax.broadcasted_iota(jnp.int32, (256, 2 * HEAD_DIM), 1) // HEAD_DIM
    causal = lax.broadcasted_iota(jnp.int32, (256, 512), 0) <= lax.rem(
        lax.broadcasted_iota(jnp.int32, (256, 512), 1), 256
    )


    def project(block):
        rows = row_block(block)
        first = scaled_rows(rows, 0, 1)
        for member, target in enumerate((q_ref, k_ref, v_ref)):
            values = nn(first, qkv_ref[member]) + qkv_bias[member : member + 1].astype(F32)
            for pair in range(heads // 2):
                lanes = slice(pair * 128, pair * 128 + 128)
                part = values[:, lanes]
                if member < 2:
                    part = rotated(part, cosine[rows, :], sine[rows, :], lane, 1.0)
                if member == 0:
                    part = part * HEAD_DIM**-0.5
                target[rows, lanes] = part.astype(BF16)
            if member == 2:
                kv_t[:, rows] = values.astype(BF16).T

    def both_heads(values):
        zero = jnp.zeros_like(values)
        return jnp.concatenate(
            [jnp.where(lane_head == 0, values, zero), jnp.where(lane_head == 1, values, zero)], 0
        )

    def own_heads(result):
        return jnp.concatenate([result[:HEAD_DIM, :256], result[HEAD_DIM:, 256:]], 0)

    def attend(block, pair):
        lanes = pl.ds(aligned(pair * 128, 128), 128)
        start = block * 256
        rows = slice(start, start + 256)
        query = both_heads(q_ref[rows, lanes])
        near = jnp.where(causal, nt(k_ref[rows, lanes], query), -jnp.inf)
        peak = jnp.max(near, 0, keepdims=True)
        if block:
            far = nt(k_ref[0:start, lanes], query)
            peak = jnp.maximum(peak, jnp.max(far, 0, keepdims=True))
        near = jnp.exp(near - peak)
        weight = jnp.sum(near, 0, keepdims=True)
        result = nn(kv_t[lanes, rows], near.astype(BF16))
        if block:
            far = jnp.exp(far - peak)
            weight = weight + jnp.sum(far, 0, keepdims=True)
            result = result + nn(kv_t[lanes, 0:start], far.astype(BF16))
        o_t[lanes, rows] = own_heads(result / weight).astype(BF16)
        lse[block, pl.ds(pair, 1)] = peak + jnp.log(weight)

    def branch_copy(block):
        rows = row_block(block)
        return remote(
            branch.at[rows], branch_other.at[rows], y_send.at[block], y_recv.at[block], place.to_y
        )

    def norm_copy(block):
        rows, at = row_block(block), blocks + block
        return remote(norm.at[rows], norm_other.at[rows], y_send.at[at], y_recv.at[at], place.to_y)

    def use_of(kind, chunk):
        return pick(chunk, [(at, use) for (name, at), use in plan.use.items() if name == kind])[0]

    def branch_share(rows, slot, chunk):
        values, share = gate(rows, slot, fc1_offset(chunk))
        branch[rows, :] += nn((values * share).astype(BF16), fc2_ref[slot])

    def first_block():
        def body(chunk, carry):
            branch_share(slice(0, 256), take_chunk(chunk), chunk)
            return carry

        lax.fori_loop(0, chunks, body, 0)

    def ahead(chunk):
        slot = take_chunk(use_of("ahead", chunk))
        branch_share(slice(256, tokens // 2), slot, chunk)
        branch_share(slice(tokens // 2, tokens), slot, chunk)

    def mix(block):
        rows = row_block(block)
        branch[rows, :] += nn(o_t[:, rows].T, dense_ref[...])
        branch_copy(block).start()

    def dense_grad(part):
        message = fc_messages + part
        slot = lax.rem(message, 4)

        stage[slot] = nn(o_t[row_block(part), :], g_ref[...])
        core_copy(message).start()

    def back_start():
        def body(index, carry):
            rows = row_block(index)
            do_ref[rows, :] = nt(g_ref[rows, :], dense_ref[...]).astype(BF16)
            kv_t[:, rows] = k_ref[rows, :].T
            return carry

        lax.fori_loop(0, blocks, body, 0)
        for row in range(8, 12):
            small[row : row + 1] = jnp.zeros((1, width), F32)
        qkv_bias_sum[...] = jnp.zeros_like(qkv_bias_sum)

    def attend_back(block, pair):
        lanes = pl.ds(aligned(pair * 128, 128), 128)
        start = block * 256
        rows = slice(start, start + 256)
        query = both_heads(q_ref[rows, lanes])
        grad = both_heads(do_ref[rows, lanes])
        stat = lse[block, pl.ds(pair, 1)]
        near = jnp.exp(jnp.where(causal, nt(k_ref[rows, lanes], query), -jnp.inf) - stat)
        near_back = nt(v_ref[rows, lanes], grad)
        centre = jnp.sum(near * near_back, 0, keepdims=True)
        if block:
            far = jnp.exp(nt(k_ref[0:start, lanes], query) - stat)
            far_back = nt(v_ref[0:start, lanes], grad)
            centre = centre + jnp.sum(far * far_back, 0, keepdims=True)

        def add(ref, here, value):
            ref[here, lanes] = value if block == blocks - 1 else ref[here, lanes] + value

        add(dv_ref, rows, nn(near.astype(BF16), grad))
        near = (near * (near_back - centre)).astype(BF16)
        add(dk_ref, rows, nn(near, query))
        result = nn(kv_t[lanes, rows], near)
        if block:
            far_rows = slice(0, start)
            add(dv_ref, far_rows, nn(far.astype(BF16), grad))
            far = (far * (far_back - centre)).astype(BF16)
            add(dk_ref, far_rows, nn(far, query))
            result = result + nn(kv_t[lanes, 0:start], far)
        dq_t[lanes, :] = own_heads(result)

    def end_rows(block):
        rows = row_block(block)
        for pair in range(heads // 2):
            lanes = slice(pair * 128, pair * 128 + 128)
            part = dq_t[lanes, :].T * HEAD_DIM**-0.5
            tables = cosine[rows, :], sine[rows, :], lane, -1.0
            q_ref[rows, lanes] = rotated(part, *tables).astype(BF16)
            k_ref[rows, lanes] = rotated(dk_ref[rows, lanes], *tables).astype(BF16)
        v_ref[rows, :] = dv_ref[rows, :].astype(BF16)
        grad = nt(q_ref[rows, :], qkv_ref[0])
        grad = grad + nt(k_ref[rows, :], qkv_ref[1])
        grad = grad + nt(v_ref[rows, :], qkv_ref[2])
        second = norm[rows, :]
        norm[rows, :] = second * vectors[2:3] + grad * vectors[0:1]
        norm_copy(block).start()
        normed, _ = normed_rows(rows)
        small[8:9] += jnp.sum(grad * normed, 0, keepdims=True)
        small[9:10] += jnp.sum(grad, 0, keepdims=True)
        small[10:11] += jnp.sum(second * normed, 0, keepdims=True)
        small[11:12] += jnp.sum(second, 0, keepdims=True)
        for member, ref in enumerate((q_ref, k_ref, v_ref)):
            qkv_bias_sum[member : member + 1] += jnp.sum(
                ref[rows, :].astype(F32), 0, keepdims=True
            )

    def transpose_first():
        def body(index, carry):
            rows = row_block(index, 128)
            ln_t[:, rows] = scaled_rows(rows, 0, 1).T
            return carry + jnp.sum(g_ref[rows, :].astype(F32), 0, keepdims=True)

        small[0:1] = lax.fori_loop(0, tokens // 128, body, jnp.zeros((1, width), F32))

    def qkv_grad(which):
        message = qkv_first + which
        slot = lax.rem(message, 4)
        first = lax.rem(which, local // 256) * 256
        for member, target in enumerate((q_ref, k_ref, v_ref)):

            @pl.when(which // (local // 256) == member)
            def _(target=target):
                for part in range(width // local):
                    left = ln_t[pl.ds(aligned(part * local + first, 256), 256), :]
                    stage[slot, :, part * local : part * local + local] = nn(left, target[...])

        core_copy(message).start()


    def small_copy():
        at = 2 * blocks
        return remote(small.at[8:16], small_y, y_send.at[at], y_recv.at[at], place.to_y)

    def small_core_copy():
        at = 2 * blocks + 1
        return remote(
            small.at[pl.ds(aligned((1 - core) * 8, 8), 8)],
            small_core,
            y_send.at[at],
            y_recv.at[at],
            place.to_core,
        )

    def gather_small():
        small[12:16] = jnp.zeros((4, width), F32)
        small[5:8] = jnp.zeros((3, width), F32)
        for part in range(hidden // CHUNK):
            row, at = part * CHUNK // width, part * CHUNK % width
            small[1 + row : 2 + row, at : at + CHUNK] = fc1_bias_sum[part : part + 1]
        small[4:5] = jnp.zeros((1, width), F32)
        for member in range(3):
            row, at = member * local // width, member * local % width
            small[3 + row : 4 + row, at : at + local] = qkv_bias_sum[member : member + 1]
        small_copy().start()

    def small_cores():
        small_copy().wait()
        small[8:16] += small_y[...]
        small_core_copy().start()

    def end_small():
        small_core_copy().wait()
        total[pl.ds(small_unit * UNIT, UNIT)] = jnp.zeros((UNIT, width), F32)
        total[pl.ds(small_unit * UNIT, 8)] = (
            small[pl.ds(aligned(core * 8, 8), 8)] + small_core[...]
        )


    def other_rows(block, src, slot):
        return pltpu.make_async_copy(src.at[row_block(block)], stage.at[slot], row_sem.at[0])

    def mixed_copy(block):
        rows = row_block(block)
        return pltpu.make_async_copy(ln_ref.at[rows], mixed_out.at[rows], row_sem.at[1 + block])

    def grad_copy(block):
        rows = row_block(block)
        return pltpu.make_async_copy(
            ln_t.at[rows], grad_out.at[rows], row_sem.at[1 + blocks + block]
        )

    def end_mixed(block):
        branch_copy(block).wait()
        copy = other_rows(block, branch_other, 0)
        copy.start()
        copy.wait()

        def body(index, carry):
            at = pl.ds(aligned(index * 64, 64), 64)
            rows = pl.ds(aligned(block * 256 + index * 64, 64), 64)
            shares = branch[rows, :] + stage[0, at]
            ln_ref[rows, :] = (
                x_ref[rows, :].astype(F32) + shares + (vectors[4:5] + vectors[5:6])
            ).astype(BF16)
            return carry

        lax.fori_loop(0, 4, body, 0)
        mixed_copy(block).start()

    def end_grad(block):
        norm_copy(block).wait()
        copy = other_rows(block, norm_other, 1)
        copy.start()
        copy.wait()

        def body(index, carry):
            at = pl.ds(aligned(index * 64, 64), 64)
            rows = pl.ds(aligned(block * 256 + index * 64, 64), 64)
            normed, inverse = normed_rows(rows)
            scaled = norm[rows, :] + stage[1, at]
            mean = jnp.mean(scaled, -1, keepdims=True)
            slope = jnp.mean(scaled * normed, -1, keepdims=True)
            ln_t[rows, :] = (
                g_ref[rows, :].astype(F32) + inverse * (scaled - mean - normed * slope)
            ).astype(BF16)
            return carry

        lax.fori_loop(0, 4, body, 0)
        grad_copy(block).start()

    def clear(index, carry):
        rows = row_block(index, 128)
        branch[rows, :] = jnp.zeros((128, width), F32)
        norm[rows, :] = jnp.zeros((128, width), F32)
        low = scaled_rows(rows, 2, 3)
        ln_ref[rows, :] = low
        ln_t[:, rows] = low.T
        return carry

    loads[0].wait()
    lax.fori_loop(0, tokens // 128, clear, 0)
    for item in loads[1:]:
        item.wait()
    place.meet()

    steps = len(plan.tasks) + units + 5 * LAG - plan.total
    mixed_at = len(plan.tasks)
    grad_at = [steps - 4 * (1 + index) for index in range(blocks)][::-1]


    def step_body(step, moved):
        message, found = pick(step, list(plan.collects.items()))

        @pl.when(found)
        def _():
            collect(message)

        moves = jnp.where(step < plan.start, 0, 1)
        for count in (0, 2):
            _, here = pick(step, [(at, 0) for at, moved in plan.moves.items() if moved == count])
            moves = jnp.where(here, count, moves)

        def move(index, carry):
            all_reduce_step(
                moved + index,
                units,
                place,
                total,
                (slot_x, slot_ae, slot_be, slot_am, slot_bm, slot_bx, slot_af),
                send,
                recv,
                finish,
            )
            return carry

        lax.fori_loop(0, moves, move, 0)

        def task(body, name, *rest):
            value, found = pick(step, plan.steps(name, *rest))

            @pl.when(found)
            def _():
                body(value)

        def full(value):
            chunk, part = value // 3, lax.rem(value, 3)
            use = use_of("full", chunk)

            @pl.when(part == 0)
            def _():
                take_chunk(use)

            @pl.when(part < 2)
            def _():
                full_body(chunk, lax.rem(use, WEIGHT_SLOTS), part)

            @pl.when(part == 2)
            def _():
                full_grads(chunk)

        task(full, "full")
        task(project, "project")
        for block in range(blocks):

            def some_heads(part, block=block):
                count = heads // 2 // FWD_PARTS[block]

                def body(index, carry):
                    attend(block, part * count + index)
                    return carry

                lax.fori_loop(0, count, body, 0)

            task(some_heads, "attend", block)
        task(lambda value: first_block(), "first")
        task(ahead, "ahead")
        task(mix, "mix")
        task(dense_grad, "dense")
        task(lambda value: back_start(), "back_start")
        for block in range(blocks):

            def some_heads_back(part, block=block):
                count = heads // 2 // BACK_PARTS[block]

                def body(index, carry):
                    attend_back(block, part * count + index)
                    return carry

                lax.fori_loop(0, count, body, 0)

            task(some_heads_back, "back", block)
        task(end_rows, "rows")
        task(lambda value: transpose_first(), "transpose")
        task(qkv_grad, "qkv")
        for part, body in enumerate((gather_small, small_cores, end_small)):

            @pl.when(step == plan.steps("small")[part][0])
            def _(body=body):
                body()

        @pl.when((step >= mixed_at) & (step < mixed_at + blocks))
        def _():
            end_mixed(step - mixed_at)

        block, found = pick(step, [(at, blocks - 1 - index) for index, at in enumerate(grad_at)])

        @pl.when(found)
        def _():
            end_grad(block)

        return moved + moves

    lax.fori_loop(0, steps, step_body, 0)

    done = total.at[pl.ds(0, small_unit * UNIT + 8)]
    pltpu.make_async_copy(done, done, out_sem.at[0]).wait()
    every = remote(done, done, out_sem.at[1], out_sem.at[2], place.to_core)
    every.wait_send()
    every.wait_recv()
    for block in range(blocks):
        mixed_copy(block).wait()
        grad_copy(block).wait()


def layer(tokens, cotangent, qkv_weight, dense_weight, fc1_weight, fc2_weight, vectors, qkv_bias):
    rows, width = tokens.shape
    local, hidden = qkv_weight.shape[2], fc1_weight.shape[1]
    cosine, sine = (jnp.asarray(table) for table in rotary_tables(rows))
    hbm = pl.BlockSpec(memory_space=pl.ANY)
    vmem = pl.BlockSpec(memory_space=pltpu.VMEM)
    quarter = UNIT // 4
    chunks = hidden // CHUNK
    blocks = rows // 256
    unit_rows = (2 * chunks + local // 256 + 3 * local // 256) * 128 + UNIT
    dma = pltpu.SemaphoreType.DMA
    scratch = [
        pltpu.VMEM((unit_rows, width), F32),
        pltpu.VMEM((4, 256, width), F32),
        pltpu.VMEM((4, 128, width), F32),
        pltpu.VMEM((SLOTS, quarter, width), F32),
        pltpu.VMEM((SLOTS, quarter, width), F32),
        pltpu.VMEM((SLOTS, 2 * quarter, width), F32),
        pltpu.VMEM((SLOTS, quarter, width), F32),
        pltpu.VMEM((SLOTS, quarter, width), F32),
        pltpu.VMEM((SLOTS, quarter, width), F32),
        pltpu.VMEM((SLOTS, quarter, width), F32),
        pltpu.VMEM((rows, width), BF16),
        pltpu.VMEM((rows, width), BF16),
        pltpu.VMEM((rows, width), BF16),
        pltpu.VMEM((width, rows), BF16),
        pltpu.VMEM((rows, width), F32),
        pltpu.VMEM((rows, width), F32),
        pltpu.VMEM((WEIGHT_SLOTS, width, CHUNK), BF16),
        pltpu.VMEM((WEIGHT_SLOTS, CHUNK, width), BF16),
        pltpu.VMEM((3, width, local), BF16),
        pltpu.VMEM((local, width), BF16),
        pltpu.VMEM((rows, local), BF16),
        pltpu.VMEM((rows, local), BF16),
        pltpu.VMEM((rows, local), BF16),
        pltpu.VMEM((local, rows), BF16),
        pltpu.VMEM((local, rows), BF16),
        pltpu.VMEM((rows, local), BF16),
        pltpu.VMEM((local, 256), F32),
        pltpu.VMEM((rows, local), F32),
        pltpu.VMEM((rows, local), F32),
        pltpu.VMEM((rows, 2 * HEAD_DIM), F32),
        pltpu.VMEM((rows, 2 * HEAD_DIM), F32),
        pltpu.VMEM((CHUNK, rows), BF16),
        pltpu.VMEM((rows, CHUNK), BF16),
        pltpu.VMEM((blocks, local // 128, 512), F32),
        pltpu.VMEM((chunks, CHUNK), F32),
        pltpu.VMEM((3, local), F32),
        pltpu.VMEM((16, width), F32),
        pltpu.VMEM((8, width), F32),
        pltpu.VMEM((8, width), F32),
        dma((10, SLOTS)),
        dma((10, SLOTS)),
        dma((4,)),
        dma((4,)),
        dma((6,)),
        dma((WEIGHT_SLOTS, 2)),
        dma((3,)),
        dma((2 * blocks + 2,)),
        dma((2 * blocks + 2,)),
        dma((1 + 2 * blocks,)),
    ]
    out = jax.ShapeDtypeStruct
    return pl.pallas_call(
        functools.partial(layer_kernel, (rows, width, local, hidden)),
        out_shape=[
            out((rows, width), BF16),
            out((rows, width), BF16),
            out((width, hidden), F32),
            out((hidden, width), F32),
            out((local, width), F32),
            out((3, width, local), F32),
            out((16, width), F32),
            out((rows, width), F32),
            out((rows, width), F32),
        ],
        in_specs=[hbm] * 6 + [vmem] * 2 + [hbm] * 2,
        out_specs=[hbm] * 9,
        scratch_shapes=scratch,
        compiler_params=pltpu.CompilerParams(
            collective_id=0, has_side_effects=True, vmem_limit_bytes=63 * 2**20
        ),
    )(
        tokens,
        cotangent,
        jnp.transpose(qkv_weight, (1, 0, 2)),
        dense_weight,
        fc1_weight,
        fc2_weight,
        vectors,
        qkv_bias,
        cosine,
        sine,
    )


def per_device(
    groups,
    tokens,
    qkv_weight,
    qkv_bias,
    dense_weight,
    dense_bias,
    fc1_weight,
    fc1_bias,
    fc2_weight,
    fc2_bias,
    ln1_gain,
    ln1_bias,
    ln2_gain,
    ln2_bias,
    cotangent,
):
    width = tokens.shape[1]
    local, hidden = qkv_weight.shape[2], fc1_weight.shape[1]
    rows_of = [ln1_gain, ln1_bias, ln2_gain, ln2_bias, dense_bias, fc2_bias]
    rows_of += [fc1_bias[at : at + width] for at in range(0, hidden, width)]
    row = lax.broadcasted_iota(jnp.int32, (len(rows_of), width), 0)
    vectors = jnp.zeros((len(rows_of), width), F32)
    for at, values in enumerate(rows_of):
        vectors = jnp.where(row == at, values.astype(F32)[None], vectors)
    mixed, input_grad, fc1_grad, fc2_grad, dense_grad, qkv_grad, small, _, _ = layer(
        tokens,
        cotangent,
        qkv_weight,
        dense_weight,
        fc1_weight,
        fc2_weight,
        vectors,
        qkv_bias,
    )
    if groups is not None:
        fc1_grad, fc2_grad, dense_grad, qkv_grad, small = lax.psum(
            (fc1_grad, fc2_grad, dense_grad, qkv_grad, small), "dp", axis_index_groups=groups
        )
    flat = small.reshape(-1)
    bias_grad = small[0]
    return (
        mixed,
        input_grad,
        jnp.transpose(qkv_grad, (1, 0, 2)),
        flat[3 * width : 3 * width + 3 * local].reshape(3, local),
        dense_grad,
        bias_grad,
        fc1_grad,
        flat[width : width + hidden],
        fc2_grad,
        bias_grad,
        small[8],
        small[9],
        small[10],
        small[11],
    )


def solution(mesh):
    dp = mesh.shape["dp"]
    groups = None
    if dp > GROUP:
        groups = [[start + i for start in range(0, dp, GROUP)] for i in range(GROUP)]
    placed = (
        P("dp", None),
        P(None, None, "tensor"),
        P(None, "tensor"),
        P("tensor", None),
        P(),
        P(None, "tensor"),
        P("tensor"),
        P("tensor", None),
        P(),
        P(),
        P(),
        P(),
        P(),
        P("dp", None),
    )
    return jax.shard_map(
        functools.partial(per_device, groups),
        mesh=mesh,
        in_specs=placed,
        out_specs=(
            P("dp", None),
            P("dp", None),
            P(None, None, "tensor"),
            P(None, "tensor"),
            P("tensor", None),
            P(),
            P(None, "tensor"),
            P("tensor"),
            P("tensor", None),
            P(),
            P(),
            P(),
            P(),
            P(),
        ),
        check_vma=False,
    )
```
